256 devices in a mesh: grp: 32 (over y, z), tpl: 8 (over x, core).
Axes of the slice: x: 4, y: 4, z: 8, core: 2. Of those that a mesh axis runs over, the one named last changes fastest.
Arguments:
- strain: bfloat16 [512, 2, 262144], P('grp', None, 'tpl'), may hold values from -6 to 6
- templates: bfloat16 [128, 2, 262144], P('grp', None, 'tpl'), may hold values from -5 to 5
- weights: float32 [3, 262144], P(None, 'tpl'), may hold values from 0.3 to 3
- detectors: int32 [512], P('grp'), may hold values from 0 to 2
- offsets: int32 [512, 4], P('grp'), may hold values from 0 to 1048448
- routes: int32 [512, 4], P('grp'), may hold values from 0 to 31, all different within a row; in each aligned block of 16 rows (0 to 15, 16 to 31, ...) at most 3 rows name the same one
Outputs:
- snr: float32 [512, 4, 4, 128], P('grp', None, None, 'tpl')
- peak: float32 [512, 4, 4], P('grp')
The draws below stay inside these ranges and needn't reach their ends.
Inputs may be any that keep to these rules, and one draw needn't show every extreme that they name: `routes`: each segment names 4 different groups. Among the 16 segments of one index of grp (aligned blocks) no group is named more than 3 times; in some blocks a group is named exactly 3 times. Every group is named somewhere.
All inputs are finite; a program needn't handle non-finite values.
Results may differ from the reference program's by a relative error of at most 0.0031.
Values may be sent and summed in bfloat16 or wider, within the bound.
A program may use at most 128 MiB of HBM per device.

```python
import math
import jax
import jax.numpy as jnp
import numpy as np
from jax import lax

FREQS = 262144
SAMPLES = 1048576
BLOCK = 256
WINDOW = 128
DETECTORS = 3
GROUP_TPL = 4
TRIGGERS = 4
SEG_DEV = 16
SEGMENTS = 512
TEMPLATES = 128
CAPACITY = 3
N_GRP = 32


def draw_templates(key, part):
    key = jax.random.fold_in(key, 11)
    freq_index = jnp.arange(FREQS, dtype=jnp.float32)
    envelope = 1.0 / jnp.sqrt(1.0 + 2.0 * freq_index / FREQS)
    values = jnp.clip(jax.random.normal(key, (TEMPLATES, 2, FREQS), jnp.float32), -5.0, 5.0)
    return (values * envelope).astype(jnp.bfloat16)


def plant(entries, rng, low, largest):
    extent = entries.shape
    index_at = [jax.random.randint(jax.random.fold_in(rng, axis), (), 0, extent[axis]) for axis in range(len(extent))]
    entries = entries.at[tuple(index_at)].set(low)
    longest = extent.index(max(extent))
    index_at[longest] = (index_at[longest] + 1) % extent[longest]
    return entries.at[tuple(index_at)].set(largest)


def steps_of(own_key, dims, pieces, least, high):
    level = 1.0
    for axis_at, parts in pieces:
        draws = jax.random.uniform(jax.random.fold_in(jax.random.fold_in(own_key, 6), axis_at), (parts,), jnp.float32, least / len(pieces), high / len(pieces))
        level = level * jnp.repeat(jnp.exp(draws), dims[axis_at] // parts).reshape((-1,) + (1,) * (len(dims) - 1 - axis_at))
    return level


def routed_block(rng, own, number, rows, amount, top, bound, lean):
    sequence = jax.random.permutation(rng, amount)
    packed, usual = load_shares(amount, rows * top, bound, lean, True), load_shares(amount, rows * top, bound, lean, False)
    places = jnp.arange(amount)

    def named(sizes, turn):
        used = int((sizes > 0).sum())
        fixed = max(1, used // 4)
        passed = fixed + (places - fixed + turn * (used - fixed)) % max(1, amount - fixed)
        return jnp.zeros((amount,), jnp.int32).at[sequence[jnp.where(places < fixed, places, passed)]].set(jnp.asarray(sizes, jnp.int32))

    sizes = jnp.where(number % 4 == 0, named(packed, number // 4), named(usual, number - number // 4 - 1))
    mixed = jax.random.permutation(jax.random.fold_in(own, 3), amount)
    source_of, receiver = mixed[0:amount // 2 * 2:2], mixed[1:amount // 2 * 2:2]
    room = jnp.minimum(sizes[source_of] - 1, bound - sizes[receiver]) // 2
    room = jnp.where((source_of == sequence[0]) | (receiver == sequence[0]) | (sizes[receiver] == 0), 0, jnp.maximum(room, 0))
    passed = jax.random.randint(jax.random.fold_in(own, 4), (amount // 2,), 0, 1 << 20) % (room + 1)
    sizes = sizes.at[source_of].add(-passed).at[receiver].add(passed)
    members = jnp.searchsorted(jnp.cumsum(sizes), jnp.arange(rows * top), side="right").astype(jnp.int32)
    table = members.reshape(top, rows).T
    table = table[jax.random.permutation(jax.random.fold_in(own, 1), rows)]
    turn = jax.random.randint(jax.random.fold_in(own, 2), (rows, 1), 0, top)
    return jnp.take_along_axis(table, (jnp.arange(top)[None, :] + turn) % top, axis=1)


def load_shares(number_of, total, bound, skew, full):
    portions = [(1 << 20) // math.isqrt(rank ** skew) + 1 for rank in range(1, number_of + 1)]
    largest = bound if full else min(bound, max(-(-total // number_of), total * portions[0] // sum(portions)))
    least = 1 if total - largest >= number_of - 1 else 0
    counts, rest = [largest] + [least] * (number_of - 1), total - largest - least * (number_of - 1)
    while rest > 0:
        free = [i for i in range(1, number_of) if counts[i] < largest] or [i for i in range(1, number_of) if counts[i] < bound]
        whole, budget = sum([portions[i] for i in free]), rest
        for i in free:
            more = min(bound - counts[i], max(1, budget * portions[i] // whole), rest)
            counts[i] = counts[i] + more
            rest = rest - more
    return np.array(counts)


def centred(key, shape, spread, limit, pieces=(), kind=jnp.bfloat16):
    values = spread * jax.random.normal(key, shape, jnp.float32)
    if pieces:
        values = values * steps_of(key, shape, pieces, -0.22, 0.18)
    return jnp.clip(values, -limit, limit).astype(kind)


def setup_inputs(seed: int = 0) -> dict:
    key_list = jax.random.split(jax.random.key(seed), 7)
    strain = centred(key_list[0], (SEGMENTS, 2, FREQS), 1.0, 6.0, ((0, 32), (2, 8)))
    templates = draw_templates(jax.random.fold_in(key_list[6], 71), 0)
    weights = jnp.clip(jnp.exp(math.log(3.0) - 2.3025851 * jax.random.uniform(key_list[2], (DETECTORS, FREQS), jnp.float32) ** steps_of(key_list[2], (DETECTORS, FREQS), ((1, 8),), -0.2, 0.2)), 0.3, 3.0)
    detectors = plant(jax.random.randint(key_list[3], (SEGMENTS,), 0, DETECTORS), jax.random.fold_in(key_list[3], 1), 0, DETECTORS - 1).astype(jnp.int32)
    offsets = plant(jax.random.randint(key_list[4], (SEGMENTS, TRIGGERS), 0, SAMPLES - WINDOW + 1), jax.random.fold_in(key_list[4], 1), 0, SAMPLES - WINDOW).astype(jnp.int32)
    routes_keys = jax.random.split(jax.random.fold_in(key_list[5], 1), SEGMENTS // SEG_DEV)
    routes_turns = jax.random.permutation(jax.random.fold_in(key_list[5], 3), SEGMENTS // SEG_DEV)
    routes = jax.vmap(lambda own, number: routed_block(jax.random.fold_in(key_list[5], 2), own, number, SEG_DEV, N_GRP, TRIGGERS, CAPACITY, 2))(routes_keys, routes_turns).reshape((SEGMENTS, TRIGGERS))
    return {"strain": strain, "templates": templates, "weights": weights, "detectors": detectors, "offsets": offsets, "routes": routes}


TWO_PI = 2.0 * math.pi
EPSILON = 1e-06

def turn_angles(freq_index, time_index, samples):
    turned = freq_index * time_index % samples
    return turned.astype(jnp.float32) * (TWO_PI / samples)

def dft_halves(block_len, window, samples):
    inside = jnp.arange(block_len, dtype=jnp.int32)[:, None]
    moment = jnp.arange(window, dtype=jnp.int32)[None, :]
    angles = turn_angles(inside, moment, samples)
    cosine = jnp.cos(angles).astype(jnp.bfloat16)
    sine_part = jnp.sin(angles).astype(jnp.bfloat16)
    upper = jnp.concatenate([cosine, sine_part], axis=1)
    lower = jnp.concatenate([-sine_part, cosine], axis=1)
    return (upper, lower)

def twiddles(first_block, block_count, block_len, window, samples):
    starts = (first_block + jnp.arange(block_count, dtype=jnp.int32)) * block_len
    moment = jnp.arange(window, dtype=jnp.int32)
    angles = turn_angles(starts[:, None], moment[None, :], samples)
    return (jnp.cos(angles), jnp.sin(angles))

def shift_rows(strain, detectors, offsets, weights, first_bin, samples):
    bins_local = strain.shape[-1]
    det_pick = (detectors[:, None] == jnp.arange(weights.shape[0], dtype=jnp.int32)[None, :]).astype(jnp.float32)
    weight_rows = jnp.dot(det_pick, weights, precision=lax.Precision.HIGHEST)
    seg_real = strain[:, 0].astype(jnp.float32) * weight_rows
    seg_imag = strain[:, 1].astype(jnp.float32) * weight_rows
    freq_index = first_bin + jnp.arange(bins_local, dtype=jnp.int32)
    angles = turn_angles(freq_index[None, None, :], offsets[:, :, None], samples)
    cosine = jnp.cos(angles)
    sine_part = jnp.sin(angles)
    real_out = seg_real[:, None] * cosine - seg_imag[:, None] * sine_part
    imag_out = seg_real[:, None] * sine_part + seg_imag[:, None] * cosine
    return jnp.stack([real_out, imag_out], axis=2).astype(jnp.bfloat16)

def filter_rows(rows_in, bank_in, upper, lower, twid_cos, twid_sin, block_len):
    seg_real = rows_in[:, None, 0].astype(jnp.float32)
    seg_imag = rows_in[:, None, 1].astype(jnp.float32)
    bank_real = bank_in[:, :, 0].astype(jnp.float32)
    bank_imag = bank_in[:, :, 1].astype(jnp.float32)
    prod_real = (seg_real * bank_real + seg_imag * bank_imag).astype(jnp.bfloat16)
    prod_imag = (seg_imag * bank_real - seg_real * bank_imag).astype(jnp.bfloat16)
    row_total, per_group, bins_local = prod_real.shape
    block_count = bins_local // block_len
    flat_real = prod_real.reshape(-1, block_len).astype(jnp.float32)
    flat_imag = prod_imag.reshape(-1, block_len).astype(jnp.float32)
    mixed = jnp.dot(flat_real, upper.astype(jnp.float32), precision=lax.Precision.HIGHEST)
    mixed = mixed + jnp.dot(flat_imag, lower.astype(jnp.float32), precision=lax.Precision.HIGHEST)
    window = upper.shape[1] // 2
    mixed = mixed.reshape(row_total, per_group, block_count, 2 * window)
    inner_real = mixed[..., :window]
    inner_imag = mixed[..., window:]
    out_real = lax.optimization_barrier(jnp.sum(inner_real * twid_cos - inner_imag * twid_sin, axis=2))
    out_imag = lax.optimization_barrier(jnp.sum(inner_real * twid_sin + inner_imag * twid_cos, axis=2))
    return jnp.stack([out_real, out_imag], axis=2)

def reference(strain, templates, weights, detectors, offsets, routes):
    upper, lower = dft_halves(BLOCK, WINDOW, SAMPLES)
    twid_cos, twid_sin = twiddles(0, FREQS // BLOCK, BLOCK, WINDOW, SAMPLES)
    power = templates[:, 0].astype(jnp.float32) ** 2 + templates[:, 1].astype(jnp.float32) ** 2
    norm_table = jnp.dot(power, (weights * weights).T, precision=lax.Precision.HIGHEST)
    norm_table = norm_table.reshape(N_GRP, GROUP_TPL, DETECTORS)
    banks = templates.reshape(N_GRP, GROUP_TPL, 2, FREQS)

    def one_segment(inputs):
        seg_row, det_row, offset_row, route_row = inputs
        shifted = shift_rows(seg_row[None], det_row[None], offset_row[None], weights, 0, SAMPLES)[0]
        chosen = jnp.take(banks, route_row, axis=0)
        series = filter_rows(shifted, chosen, upper, lower, twid_cos, twid_sin, BLOCK)
        magnitude = jnp.sqrt(series[:, :, 0] ** 2 + series[:, :, 1] ** 2)
        norm_rows = jnp.take(norm_table, route_row, axis=0)
        det_pick = (det_row == jnp.arange(DETECTORS, dtype=jnp.int32)).astype(jnp.float32)
        root_norm = jnp.sqrt(lax.optimization_barrier(jnp.sum(norm_rows * det_pick, axis=-1)) + EPSILON)
        return (magnitude / root_norm[..., None], lax.optimization_barrier(jnp.max(magnitude, axis=-1)) / root_norm)
    snr, peak = lax.map(one_segment, (strain, detectors, offsets, routes))
    return (snr, peak)
```

```python
import functools
import math

import jax
import jax.numpy as jnp
from jax import lax
from jax.experimental import pallas as pl
from jax.experimental.pallas import tpu as pltpu
from jax.sharding import Mesh
from jax.sharding import PartitionSpec as P

SAMPLES = 1048576
WINDOW = 128
CHUNK = 256
TWO_PI = 2.0 * math.pi
EPSILON = 1e-06


def turns(index, moment):
    angles = (index * moment % SAMPLES).astype(jnp.float32) * (TWO_PI / SAMPLES)
    return jnp.cos(angles), jnp.sin(angles)


def filter_kernel(
    seg_ref, bank_ref, wgt_ref, det_ref, pick_ref, base_ref, step_ref, inner_ref, outer_ref,
    acc_ref, norm_ref, phase_ref,
):
    chunk = pl.program_id(0)

    @pl.when(chunk == 0)
    def _():
        phase_ref[...] = base_ref[...]
        acc_ref[...] = jnp.zeros_like(acc_ref)
        norm_ref[...] = jnp.zeros_like(norm_ref)

    det = det_ref[...]
    wgt = wgt_ref[...]
    chosen = jnp.where(det == 0, wgt[0:1], jnp.where(det == 1, wgt[1:2], wgt[2:3]))
    seg_re = seg_ref[0].astype(jnp.float32) * chosen
    seg_im = seg_ref[1].astype(jnp.float32) * chosen
    rows, width = phase_ref.shape[1], phase_ref.shape[2]
    segs = seg_re.shape[0]
    per = rows // segs
    cos_p = phase_ref[0]
    sin_p = phase_ref[1]
    cos_k = cos_p.reshape(per, segs, width)
    sin_k = sin_p.reshape(per, segs, width)
    sh_re = (seg_re[None] * cos_k - seg_im[None] * sin_k).astype(jnp.bfloat16)
    sh_im = (seg_re[None] * sin_k + seg_im[None] * cos_k).astype(jnp.bfloat16)
    sh_re = sh_re.astype(jnp.float32).reshape(rows, width)
    sh_im = sh_im.astype(jnp.float32).reshape(rows, width)
    cos_s = step_ref[0]
    sin_s = step_ref[1]
    phase_ref[0] = cos_p * cos_s - sin_p * sin_s
    phase_ref[1] = cos_p * sin_s + sin_p * cos_s

    cos_b = outer_ref[0, 0]
    sin_b = outer_ref[0, 1]
    cos_a = inner_ref[0]
    sin_a = inner_ref[1]
    cos_e = (cos_a * cos_b - sin_a * sin_b).astype(jnp.bfloat16)
    sin_e = (sin_a * cos_b + cos_a * sin_b).astype(jnp.bfloat16)
    upper = jnp.concatenate([cos_e, sin_e], axis=1)
    lower = jnp.concatenate([-sin_e, cos_e], axis=1)

    bank_re = bank_ref[0]
    bank_im = bank_ref[1]
    for m in range(acc_ref.shape[0] // rows):
        span = slice(m * rows, (m + 1) * rows)
        pick = pick_ref[span]
        got_re = jnp.dot(pick, bank_re, preferred_element_type=jnp.float32)
        got_im = jnp.dot(pick, bank_im, preferred_element_type=jnp.float32)
        prod_re = (sh_re * got_re + sh_im * got_im).astype(jnp.bfloat16)
        prod_im = (sh_im * got_re - sh_re * got_im).astype(jnp.bfloat16)
        acc_ref[span] += jnp.dot(
            prod_re, upper, preferred_element_type=jnp.float32
        ) + jnp.dot(prod_im, lower, preferred_element_type=jnp.float32)

    power = bank_re.astype(jnp.float32) ** 2 + bank_im.astype(jnp.float32) ** 2
    for d in range(norm_ref.shape[0]):
        scaled = power * (wgt[d : d + 1] * wgt[d : d + 1])
        norm_ref[d] += scaled[:, :128] + scaled[:, 128:]


def filter_bins(seg, bank, wgt, det, pick, base, step, inner, outer):
    bins = seg.shape[-1]
    chunks = bins // CHUNK
    whole = lambda shape: pl.BlockSpec(shape, lambda c: (0,) * len(shape))
    along = lambda shape: pl.BlockSpec(shape, lambda c: (0,) * (len(shape) - 1) + (c,))
    total = pick.shape[0]
    flops = 2 * total * bins * (256 + 512)
    return pl.pallas_call(
        filter_kernel,
        grid=(chunks,),
        in_specs=[
            along((2, seg.shape[1], CHUNK)),
            along((2, bank.shape[1], CHUNK)),
            along((wgt.shape[0], CHUNK)),
            whole(det.shape),
            whole(pick.shape),
            whole(base.shape),
            whole(step.shape),
            whole(inner.shape),
            pl.BlockSpec((1, 2, 1, WINDOW), lambda c: (c, 0, 0, 0)),
        ],
        out_specs=[
            whole((total, 2 * WINDOW)),
            whole((wgt.shape[0], bank.shape[1], 128)),
        ],
        out_shape=[
            jax.ShapeDtypeStruct((total, 2 * WINDOW), jnp.float32),
            jax.ShapeDtypeStruct((wgt.shape[0], bank.shape[1], 128), jnp.float32),
        ],
        scratch_shapes=[pltpu.VMEM(base.shape, jnp.float32)],
        compiler_params=pltpu.CompilerParams(vmem_limit_bytes=48 * 1024 * 1024),
        cost_estimate=pl.CostEstimate(flops=flops, bytes_accessed=8 << 20, transcendentals=0),
    )(seg, bank, wgt, det, pick, base, step, inner, outer)


def body(strain, templates, weights, detectors, offsets, routes):
    home_segs, triggers = routes.shape
    per_group = templates.shape[0]
    ny = lax.axis_size("y")
    nz = lax.axis_size("z")
    bins = strain.shape[-1] // ny
    y = lax.axis_index("y")
    first = (lax.axis_index("x") * lax.axis_size("core") + lax.axis_index("core")) * strain.shape[-1] + y * bins

    seg = lax.all_to_all(strain, "y", split_axis=2, concat_axis=0, tiled=True)
    seg = seg.transpose(1, 0, 2)
    bank = lax.all_to_all(templates, "y", split_axis=2, concat_axis=0, tiled=True)
    bank = lax.all_gather(bank, "z", axis=0, tiled=False)
    bank = bank.reshape(nz, ny, per_group, 2, bins).transpose(3, 1, 0, 2, 4).reshape(2, -1, bins)
    wgt = lax.dynamic_slice_in_dim(weights, y * bins, bins, 1)
    det = lax.all_gather(detectors, "y", axis=0, tiled=True)
    off = lax.all_gather(offsets, "y", axis=0, tiled=True)
    rts = lax.all_gather(routes, "y", axis=0, tiled=True)
    segs = det.shape[0]
    rows = segs * triggers
    off_rows = off.T.reshape(rows, 1)
    rts_rows = rts.T.reshape(rows)

    lanes = jnp.arange(CHUNK, dtype=jnp.int32)
    base = jnp.stack(turns(off_rows, first + lanes[None, :]))
    step = jnp.stack(turns(off_rows, jnp.full((1, CHUNK), CHUNK, jnp.int32)))
    moment = jnp.arange(WINDOW, dtype=jnp.int32)
    inner = jnp.stack(turns(lanes[:, None], moment[None, :]))
    starts = first + CHUNK * jnp.arange(bins // CHUNK, dtype=jnp.int32)
    outer = jnp.stack(turns(starts[:, None], moment[None, :]), axis=1)[:, :, None, :]
    names = (rts_rows[None, :] * per_group + jnp.arange(per_group, dtype=jnp.int32)[:, None]).reshape(-1, 1)
    pick = (names == jnp.arange(bank.shape[1], dtype=jnp.int32)[None, :]).astype(jnp.bfloat16)

    acc, norm = filter_bins(seg, bank, wgt, det[:, None], pick, base, step, inner, outer)

    acc = acc.reshape(per_group * triggers, ny, home_segs * 2 * WINDOW)
    own = lax.psum_scatter(acc, "y", scatter_dimension=1, tiled=False)
    own = lax.psum(own, ("x", "core")).reshape(per_group, triggers, home_segs, 2 * WINDOW)
    norm = lax.psum(jnp.sum(norm, axis=-1), ("y", "x", "core"))
    magnitude = jnp.sqrt(own[..., :WINDOW] ** 2 + own[..., WINDOW:] ** 2)
    magnitude = magnitude.transpose(2, 1, 0, 3)
    peak = jnp.max(magnitude, axis=-1)
    part = lax.axis_size("x") * lax.axis_size("core")
    width = WINDOW // part
    at = lax.axis_index("x") * lax.axis_size("core") + lax.axis_index("core")
    mine = lax.dynamic_slice_in_dim(magnitude, at * width, width, 3)
    table = norm.reshape(norm.shape[0], -1, per_group)
    det_pick = (detectors[:, None] == jnp.arange(norm.shape[0], dtype=jnp.int32)).astype(jnp.float32)
    grp_pick = (routes[:, :, None] == jnp.arange(table.shape[1], dtype=jnp.int32)).astype(jnp.float32)
    by_det = jnp.sum(det_pick[:, :, None, None] * table[None], axis=1)
    power = jnp.sum(grp_pick[..., None] * by_det[:, None], axis=2)
    root = jnp.sqrt(power + EPSILON)
    return mine / root[..., None], peak / root


def solution(mesh):
    ny = 4
    devices = mesh.devices
    nz = devices.shape[0] // ny
    fine = Mesh(devices.reshape(ny, nz, devices.shape[1] // 2, 2), ("y", "z", "x", "core"))
    grp, tpl = ("y", "z"), ("x", "core")
    return jax.shard_map(
        body,
        mesh=fine,
        in_specs=(
            P(grp, None, tpl),
            P(grp, None, tpl),
            P(None, tpl),
            P(grp),
            P(grp, None),
            P(grp, None),
        ),
        out_specs=(P(grp, None, None, tpl), P(grp, None, None)),
        check_vma=False,
    )
```

```python
import functools
import math

import jax
import jax.numpy as jnp
from jax import lax
from jax.experimental import pallas as pl
from jax.experimental.pallas import tpu as pltpu
from jax.sharding import Mesh
from jax.sharding import PartitionSpec as P

SAMPLES = 1048576
WINDOW = 128
LANES = 128
CHUNK = 2 * LANES
LAG = 2
BANK_PARTS = 4
SEG_PARTS = 8
TWO_PI = 2.0 * math.pi
EPSILON = 1e-06
MESH = pl.DeviceIdType.MESH


def turns(index, moment):
    angles = ((index * moment) & (SAMPLES - 1)).astype(jnp.float32) * (TWO_PI / SAMPLES)
    return jnp.cos(angles), jnp.sin(angles)


def iota(shape, dim):
    return lax.broadcasted_iota(jnp.int32, shape, dim)


def filter_kernel(
    dims, strain, bank, meta, wgt, snr, peak,
    stage_b, stage_s, bank_buf, seg_buf, meta_buf, pick, perm, phase, step, inner, outer,
    acc, norm, nsum, r0, n0, r1, n1, mags,
    bank_load, bank_own, seg_load, yb_send, yb_recv, ys_send, ys_recv, meta_send, meta_recv,
    z_send, z_recv, r0_send, r0_recv, r1_send, r1_recv, r2_send, r2_recv,
):
    nx, ny, nz = dims
    x, y, z, core = (lax.axis_index(a) for a in ("x", "y", "z", "core"))
    home, triggers = strain.shape[0], 4
    per_group = bank.shape[0]
    blocks = bank_buf.shape[0]
    chunks = blocks // 2
    segs = home * ny
    rows = segs * triggers
    names = nz * ny * per_group
    pairs = per_group * triggers
    half = pairs // 2
    share = half // nx
    reach = nz // 2
    bins = blocks * LANES
    first = ((x * 2 + core) * ny + y) * bins
    bank_rows = blocks // BANK_PARTS
    seg_rows = blocks // SEG_PARTS
    up, down = lax.rem(z + 1, nz), lax.rem(z + nz - 1, nz)

    def remote(src, dst, send, recv, where):
        return pltpu.make_async_remote_copy(
            src_ref=src, dst_ref=dst, send_sem=send, recv_sem=recv, device_id=where, device_id_type=MESH
        )

    def other_y(shift):
        return lax.rem(y + shift, ny)

    for m in range(per_group):
        pltpu.make_async_copy(bank.at[m], stage_b.at[:, m], bank_load).start()
    for shift in list(range(1, ny)) + [0]:
        span = pl.ds(other_y(shift) * blocks, blocks)

        def load(s, carry, shift=shift, span=span):
            if shift:
                dst = stage_s.at[shift - 1, :, s]
            else:
                dst = seg_buf.at[:, y * home + s]
            pltpu.make_async_copy(strain.at[s, span], dst, seg_load.at[shift]).start()
            return carry

        lax.fori_loop(0, home, load, 0)

    barrier = pltpu.get_barrier_semaphore()
    plane = [(dx, dy) for dx in range(nx) for dy in range(ny) if dx or dy]
    tpl = [(dx, dc) for dx in range(nx) for dc in range(2) if dx or dc]

    def at_plane(dx, dy):
        return {"x": lax.rem(x + dx, nx), "y": lax.rem(y + dy, ny)}

    def at_tpl(dx, dc):
        return {"x": lax.rem(x + dx, nx), "core": lax.rem(core + dc, 2)}

    greeted = [at_plane(dx, dy) for dx, dy in plane]
    greeted += [at_tpl(dx, dc) for dx, dc in tpl if dc]
    greeted += [{"z": up}, {"z": down}]
    for who in greeted:
        pl.semaphore_signal(barrier, inc=1, device_id=who, device_id_type=MESH)

    cos_a, sin_a = turns(iota((CHUNK, WINDOW), 0), iota((CHUNK, WINDOW), 1))
    inner[0] = cos_a
    inner[1] = sin_a
    cos_b, sin_b = turns(first + CHUNK * iota((chunks, WINDOW), 0), iota((chunks, WINDOW), 1))
    outer[0] = cos_b
    outer[1] = sin_b
    wanted = iota((2 * segs, 2 * segs), 0)
    wanted = jnp.where(wanted < segs, 2 * wanted, 2 * (wanted - segs) + 1)
    perm[...] = jnp.where(wanted == iota((2 * segs, 2 * segs), 1), 1.0, 0.0).astype(jnp.bfloat16)
    meta_buf[y] = meta[...]

    pltpu.make_async_copy(stage_b, stage_b, bank_load).wait()
    own_bank = pltpu.make_async_copy(
        stage_b.at[pl.ds(y * blocks, blocks)], bank_buf.at[:, z, pl.ds(y * per_group, per_group)], bank_own
    )
    own_bank.start()
    pl.semaphore_wait(barrier, len(greeted))

    def bank_part(part, shift):
        span = pl.ds(part * bank_rows, bank_rows)
        return remote(
            stage_b.at[pl.ds(other_y(shift) * blocks + part * bank_rows, bank_rows)],
            bank_buf.at[span, z, pl.ds(y * per_group, per_group)],
            yb_send.at[shift - 1], yb_recv.at[part, shift - 1], {"y": other_y(shift)},
        )

    def meta_part(shift):
        return remote(
            meta, meta_buf.at[y], meta_send.at[shift - 1], meta_recv.at[shift - 1], {"y": other_y(shift)}
        )

    def seg_part(part, shift):
        span = pl.ds(part * seg_rows, seg_rows)
        return remote(
            stage_s.at[shift - 1, span], seg_buf.at[span, pl.ds(y * home, home)],
            ys_send.at[shift - 1], ys_recv.at[part, shift - 1], {"y": other_y(shift)},
        )

    for shift in range(1, ny):
        bank_part(0, shift).start()
    for shift in range(1, ny):
        meta_part(shift).start()
    for part in range(1, BANK_PARTS):
        for shift in range(1, ny):
            bank_part(part, shift).start()
    for shift in range(1, ny):
        pltpu.make_async_copy(stage_s.at[shift - 1], stage_s.at[shift - 1], seg_load.at[shift]).wait()

    def send_segs(part, carry):
        for shift in range(1, ny):
            seg_part(part, shift).start()
        return carry

    lax.fori_loop(0, SEG_PARTS, send_segs, 0)
    own_bank.wait()

    def hop(chunk, h, rise):
        origin = lax.rem(z + (nz - h + 1 if rise else h - 1), nz)
        ref = bank_buf.at[pl.ds(2 * chunk, 2), origin]
        way = 0 if rise else 1
        return remote(
            ref, ref, z_send.at[way, h - 1], z_recv.at[way, h - 1, chunk], {"z": up if rise else down}
        )

    def landed(chunk, h, rise):
        origin = lax.rem(z + (nz - h if rise else h), nz)
        ref = bank_buf.at[pl.ds(2 * chunk, 2), origin]
        way = 0 if rise else 1
        remote(
            ref, ref, z_send.at[way, h - 1], z_recv.at[way, h - 1, chunk], {"z": up if rise else down}
        ).wait_recv()

    def when(cond, run):
        if isinstance(cond, bool):
            if cond:
                run()
        else:
            pl.when(cond)(run)

    def both(a, b):
        if isinstance(a, bool):
            return a and b
        return jnp.logical_and(a, b)

    def tick(t):
        def last(chunk=t - LAG * reach):
            def go():
                when(chunk % 2 == 0, lambda: landed(chunk, reach, True))
                when(chunk % 2 == 1, lambda: landed(chunk, reach, False))

            when(both(chunk >= 0, chunk < chunks), go)

        last()
        for h in range(reach, 0, -1):
            chunk = t - LAG * (h - 1)

            def go(chunk=chunk, h=h):
                if h > 1:
                    landed(chunk, h - 1, True)
                    landed(chunk, h - 1, False)
                else:
                    per_part = bank_rows // 2

                    def arrived():
                        for shift in range(1, ny):
                            bank_part(chunk // per_part, shift).wait_recv()

                    when(chunk % per_part == 0, arrived)
                if h < reach:
                    hop(chunk, h, True).start()
                    hop(chunk, h, False).start()
                else:
                    when(chunk % 2 == 0, lambda: hop(chunk, h, True).start())
                    when(chunk % 2 == 1, lambda: hop(chunk, h, False).start())

            when(both(chunk >= 0, chunk < chunks), go)

    def tables_phase(k):
        info = meta_buf[...].reshape(segs, LANES)
        off = info[:, 1 + k : 2 + k]
        cos_p, sin_p = turns(off, first + iota((segs, CHUNK), 1))
        phase[0, k * segs : (k + 1) * segs] = cos_p
        phase[1, k * segs : (k + 1) * segs] = sin_p
        cos_s, sin_s = turns(off, jnp.full((segs, LANES), CHUNK, jnp.int32))
        step[0, k * segs : (k + 1) * segs] = cos_s
        step[1, k * segs : (k + 1) * segs] = sin_s

    def tables_pick(k):
        info = meta_buf[...].reshape(segs, LANES)
        grp = info[:, 5 + k : 6 + k]
        spot = 2 * per_group * (lax.rem(grp, nz) * ny + lax.div(grp, nz))
        spot = jnp.broadcast_to(spot, (segs, 2 * names)) - iota((segs, 2 * names), 1)
        for m in range(per_group):
            to = slice((m * triggers + k) * segs, (m * triggers + k + 1) * segs)
            for part in range(2):
                hit = spot == -(2 * m + part)
                pick[part, to] = jnp.where(hit, 1.0, 0.0).astype(jnp.bfloat16)

    acc[...] = jnp.zeros_like(acc)
    norm[...] = jnp.zeros_like(norm)
    ramp = LAG * reach
    for t in range(ramp):
        tick(t)
        if t == 1:
            for shift in range(1, ny):
                meta_part(shift).wait_recv()
        for k in range(triggers):
            if t == 2 + k % (ramp - 2):
                tables_phase(k)
                tables_pick(k)
    pltpu.make_async_copy(
        seg_buf.at[:, pl.ds(y * home, home)], seg_buf.at[:, pl.ds(y * home, home)], seg_load.at[0]
    ).wait()

    def filter_chunk(c):
        per_part = seg_rows // 2

        def arrived():
            for shift in range(1, ny):
                seg_part(c // per_part, shift).wait_recv()

        pl.when(c % per_part == 0)(arrived)
        seg = jnp.concatenate([seg_buf[2 * c + i].reshape(2 * segs, LANES) for i in range(2)], axis=1)
        got = jnp.concatenate([bank_buf[2 * c + i].reshape(2 * names, LANES) for i in range(2)], axis=1)
        seg = jnp.dot(perm[...], seg, preferred_element_type=jnp.float32)
        w = wgt[:, pl.ds(pl.multiple_of(y * bins + c * CHUNK, CHUNK), CHUNK)]
        det = meta_buf[...].reshape(segs, LANES)[:, 0:1]
        chosen = jnp.where(det == 0, w[0:1], jnp.where(det == 1, w[1:2], w[2:3]))
        seg_re = (seg[:segs] * chosen)[None]
        seg_im = (seg[segs:] * chosen)[None]
        cos_p = phase[0]
        sin_p = phase[1]
        cos_k = cos_p.reshape(triggers, segs, CHUNK)
        sin_k = sin_p.reshape(triggers, segs, CHUNK)
        sh_re = (seg_re * cos_k - seg_im * sin_k).astype(jnp.bfloat16).astype(jnp.float32).reshape(rows, CHUNK)
        sh_im = (seg_re * sin_k + seg_im * cos_k).astype(jnp.bfloat16).astype(jnp.float32).reshape(rows, CHUNK)
        cos_s = jnp.concatenate([step[0], step[0]], axis=1)
        sin_s = jnp.concatenate([step[1], step[1]], axis=1)
        phase[0] = cos_p * cos_s - sin_p * sin_s
        phase[1] = cos_p * sin_s + sin_p * cos_s

        cos_b = outer[0, pl.ds(c, 1)]
        sin_b = outer[1, pl.ds(c, 1)]
        cos_e = (inner[0] * cos_b - inner[1] * sin_b).astype(jnp.bfloat16)
        sin_e = (inner[1] * cos_b + inner[0] * sin_b).astype(jnp.bfloat16)
        upper = jnp.concatenate([cos_e, sin_e], axis=1)
        lower = jnp.concatenate([-sin_e, cos_e], axis=1)
        for m in range(per_group):
            span = slice(m * rows, (m + 1) * rows)
            got_re = jnp.dot(pick[0, span], got, preferred_element_type=jnp.float32)
            got_im = jnp.dot(pick[1, span], got, preferred_element_type=jnp.float32)
            prod_re = (sh_re * got_re + sh_im * got_im).astype(jnp.bfloat16)
            prod_im = (sh_im * got_re - sh_re * got_im).astype(jnp.bfloat16)
            term = jnp.dot(prod_re, upper, preferred_element_type=jnp.float32)
            term = term + jnp.dot(prod_im, lower, preferred_element_type=jnp.float32)
            acc[m * triggers : (m + 1) * triggers] += term.reshape(triggers, segs, 2 * WINDOW)
        power = got.astype(jnp.float32)
        power = power * power
        for d in range(norm.shape[0]):
            scaled = power * (w[d : d + 1] * w[d : d + 1])
            norm[d] += scaled[:, :LANES] + scaled[:, LANES:]

    def advance(t, carry):
        tick(t)
        filter_chunk(t - ramp)
        return carry

    lax.fori_loop(ramp, chunks + ramp, advance, 0)

    mine = pl.ds(core * half, half)
    theirs = pl.ds((1 - core) * half, half)
    core_part = remote(acc.at[theirs], r0, r0_send.at[0], r0_recv.at[0], {"core": 1 - core})
    core_part.start()
    ones = jnp.ones((8, LANES), jnp.float32)
    for d in range(norm.shape[0]):
        line = lax.dot_general(
            ones, norm[d], (((1,), (1,)), ((), ())),
            precision=lax.Precision.HIGHEST, preferred_element_type=jnp.float32,
        )
        nsum[d : d + 1] = line[0:1]
    nsum[norm.shape[0] :] = jnp.zeros((8 - norm.shape[0], 2 * names), jnp.float32)
    core_norm = remote(nsum, n0, r0_send.at[1], r0_recv.at[1], {"core": 1 - core})
    core_norm.start()
    core_part.wait()
    acc[mine] = acc[mine] + r0[...]
    core_norm.wait()
    nsum[...] = nsum[...] + n0[...]

    def plane_part(i, dx, dy):
        who = at_plane(dx, dy)
        return remote(
            acc.at[pl.ds(core * half + who["x"] * share, share), pl.ds(who["y"] * home, home)],
            r1.at[i], r1_send.at[0, i], r1_recv.at[0, i], who,
        )

    def plane_norm(i, dx, dy):
        return remote(nsum, n1.at[i], r1_send.at[1, i], r1_recv.at[1, i], at_plane(dx, dy))

    for i, (dx, dy) in enumerate(plane):
        plane_part(i, dx, dy).start()
    for i, (dx, dy) in enumerate(plane):
        plane_norm(i, dx, dy).start()
    own = pl.ds(core * half + x * share, share)
    total = acc[own, pl.ds(pl.multiple_of(y * home, home), home)]
    for i, (dx, dy) in enumerate(plane):
        plane_part(i, dx, dy).wait_recv()
        total = total + r1[i]
    mags[own] = jnp.sqrt(total[:, :, :WINDOW] ** 2 + total[:, :, WINDOW:] ** 2)

    def tpl_part(i, dx, dc):
        return remote(mags.at[own], mags.at[own], r2_send.at[i], r2_recv.at[i], at_tpl(dx, dc))

    def tpl_landed(i, dx, dc):
        spot = lax.rem(core + dc, 2) * half + lax.rem(x + nx - dx, nx) * share
        ref = mags.at[pl.ds(spot, share)]
        remote(ref, ref, r2_send.at[i], r2_recv.at[i], at_tpl(dx, dc)).wait_recv()

    for i, (dx, dc) in enumerate(tpl):
        tpl_part(i, dx, dc).start()
    table = nsum[...]
    for i, (dx, dy) in enumerate(plane):
        plane_norm(i, dx, dy).wait_recv()
        table = table + n1[i]
    info = meta[...]
    det = info[:, 0:1]
    chosen = jnp.where(det == 0, table[0:1], jnp.where(det == 1, table[1:2], table[2:3]))
    place = lax.shift_right_logical(iota((home, 2 * names), 1), 1)
    roots = {}
    for k in range(triggers):
        grp = info[:, 5 + k : 6 + k]
        spot = per_group * (lax.rem(grp, nz) * ny + lax.div(grp, nz))
        for m in range(per_group):
            value = jnp.sum(jnp.where(place == spot + m, chosen, 0.0), axis=1, keepdims=True)
            roots[m * triggers + k] = jnp.sqrt(value + EPSILON)
    for i, (dx, dc) in enumerate(tpl):
        tpl_landed(i, dx, dc)
    for pair in range(pairs):
        level = mags[pair]
        snr[pair] = level / roots[pair]
        peak[pair] = jnp.max(level, axis=1, keepdims=True) / roots[pair]

    for shift in range(1, ny):
        remote(stage_b.at[pl.ds(0, blocks)], stage_b.at[pl.ds(0, blocks)], yb_send.at[shift - 1],
               yb_recv.at[0, shift - 1], {"y": other_y(shift)}).wait_send()
        meta_part(shift).wait_send()
        remote(stage_s.at[shift - 1], stage_s.at[shift - 1], ys_send.at[shift - 1],
               ys_recv.at[0, shift - 1], {"y": other_y(shift)}).wait_send()
    for way in range(2):
        for h in range(1, reach + 1):
            ref = bank_buf.at[:, 0] if h < reach else bank_buf.at[pl.ds(0, blocks // 2), 0]
            remote(ref, ref, z_send.at[way, h - 1], z_recv.at[way, h - 1, 0], {"z": up}).wait_send()
    for i, (dx, dy) in enumerate(plane):
        plane_part(i, dx, dy).wait_send()
        plane_norm(i, dx, dy).wait_send()
    for i, (dx, dc) in enumerate(tpl):
        tpl_part(i, dx, dc).wait_send()


def filter_bins(dims, strain, bank, meta, wgt):
    nx, ny, nz = dims
    home, whole_blocks = strain.shape[0], strain.shape[1]
    per_group = bank.shape[0]
    blocks = whole_blocks // ny
    chunks = blocks // 2
    segs, triggers = home * ny, 4
    rows = segs * triggers
    names = nz * ny * per_group
    pairs = per_group * triggers
    half = pairs // 2
    share = half // nx
    near = nx * ny - 1
    reach = nz // 2
    dets = wgt.shape[0]
    f32, bf16 = jnp.float32, jnp.bfloat16
    dma = pltpu.SemaphoreType.DMA
    total = rows * per_group
    any_space = pl.BlockSpec(memory_space=pl.ANY)
    vmem = pl.BlockSpec(memory_space=pltpu.VMEM)
    return pl.pallas_call(
        functools.partial(filter_kernel, dims),
        in_specs=[any_space, any_space, vmem, vmem],
        out_specs=[vmem, vmem],
        out_shape=[
            jax.ShapeDtypeStruct((pairs, home, WINDOW), f32),
            jax.ShapeDtypeStruct((pairs, home, 1), f32),
        ],
        scratch_shapes=[
            pltpu.VMEM((whole_blocks, per_group, 2, LANES), bf16),
            pltpu.VMEM((ny - 1, blocks, home, 2, LANES), bf16),
            pltpu.VMEM((blocks, nz, ny * per_group, 2, LANES), bf16),
            pltpu.VMEM((blocks, segs, 2, LANES), bf16),
            pltpu.VMEM((ny, home, LANES), jnp.int32),
            pltpu.VMEM((2, total, 2 * names), bf16),
            pltpu.VMEM((2 * segs, 2 * segs), bf16),
            pltpu.VMEM((2, rows, CHUNK), f32),
            pltpu.VMEM((2, rows, LANES), f32),
            pltpu.VMEM((2, CHUNK, WINDOW), f32),
            pltpu.VMEM((2, chunks, WINDOW), f32),
            pltpu.VMEM((pairs, segs, 2 * WINDOW), f32),
            pltpu.VMEM((dets, 2 * names, LANES), f32),
            pltpu.VMEM((8, 2 * names), f32),
            pltpu.VMEM((half, segs, 2 * WINDOW), f32),
            pltpu.VMEM((8, 2 * names), f32),
            pltpu.VMEM((near, share, home, 2 * WINDOW), f32),
            pltpu.VMEM((near, 8, 2 * names), f32),
            pltpu.VMEM((pairs, home, WINDOW), f32),
            dma, dma, dma((ny,)),
            dma((ny - 1,)), dma((BANK_PARTS, ny - 1)),
            dma((ny - 1,)), dma((SEG_PARTS, ny - 1)),
            dma((ny - 1,)), dma((ny - 1,)),
            dma((2, reach)), dma((2, reach, chunks)),
            dma((2,)), dma((2,)),
            dma((2, near)), dma((2, near)),
            dma((2 * nx - 1,)), dma((2 * nx - 1,)),
        ],
        compiler_params=pltpu.CompilerParams(
            collective_id=0, has_side_effects=True, vmem_limit_bytes=56 * 1024 * 1024
        ),
        cost_estimate=pl.CostEstimate(
            flops=2 * total * blocks * LANES * 1024, bytes_accessed=4 << 20, transcendentals=0
        ),
    )(strain, bank, meta, wgt)


def body(dims, strain, templates, weights, detectors, offsets, routes):
    nx = dims[0]
    home, triggers = routes.shape

    def by_blocks(a):
        return a.reshape(a.shape[0], 2, -1, LANES).transpose(0, 2, 1, 3)

    meta = jnp.concatenate([detectors[:, None], offsets, routes], axis=1)
    meta = jnp.pad(meta, ((0, 0), (0, LANES - meta.shape[1])))
    snr, peak = filter_bins(dims, by_blocks(strain), by_blocks(templates), meta, weights)
    width = WINDOW // (2 * nx)
    at = lax.axis_index("x") * 2 + lax.axis_index("core")
    snr = lax.dynamic_slice_in_dim(snr, at * width, width, 2)
    snr = snr.reshape(-1, triggers, home, width).transpose(2, 1, 0, 3)
    peak = peak.reshape(-1, triggers, home).transpose(2, 1, 0)
    return snr, peak


def solution(mesh):
    devices = mesh.devices
    ny = 4 if devices.shape[0] % 4 == 0 and devices.shape[0] > 8 else 2
    nz = devices.shape[0] // ny
    nx = devices.shape[1] // 2
    fine = Mesh(devices.reshape(ny, nz, nx, 2), ("y", "z", "x", "core"))
    grp, tpl = ("y", "z"), ("x", "core")
    return jax.shard_map(
        functools.partial(body, (nx, ny, nz)),
        mesh=fine,
        in_specs=(
            P(grp, None, tpl),
            P(grp, None, tpl),
            P(None, tpl),
            P(grp),
            P(grp, None),
            P(grp, None),
        ),
        out_specs=(P(grp, None, None, tpl), P(grp, None, None)),
        check_vma=False,
    )
```

```python
import functools
import math

import jax
import jax.numpy as jnp
from jax import lax
from jax.experimental import pallas as pl
from jax.experimental.pallas import tpu as pltpu
from jax.sharding import Mesh
from jax.sharding import PartitionSpec as P

SAMPLES = 1048576
WINDOW = 128
LANES = 128
CHUNK = 2 * LANES
PIECE = 2
LAG = 2
BURST = 4
BANK_PARTS = 4
SEG_PARTS = 8
TWO_PI = 2.0 * math.pi
EPSILON = 1e-06
MESH = pl.DeviceIdType.MESH


def turns(index, moment):
    angles = ((index * moment) & (SAMPLES - 1)).astype(jnp.float32) * (TWO_PI / SAMPLES)
    return jnp.cos(angles), jnp.sin(angles)


def iota(shape, dim):
    return lax.broadcasted_iota(jnp.int32, shape, dim)


def filter_kernel(
    dims, strain, bank, meta, wgt, snr, peak,
    stage_b, stage_s, bank_buf, seg_buf, meta_buf, pick, perm, phase, step, inner, outer,
    acc, norm, nsum, r0, n0, r1, n1, mags,
    bank_load, bank_own, seg_load, yb_send, yb_recv, ys_send, ys_recv, meta_send, meta_recv,
    z_send, z_recv, r0_send, r0_recv, r1_send, r1_recv, r2_send, r2_recv,
):
    nx, ny, nz = dims
    x, y, z, core = (lax.axis_index(a) for a in ("x", "y", "z", "core"))
    home, triggers = strain.shape[0], 4
    per_group = bank.shape[0]
    blocks = bank_buf.shape[0]
    chunks = blocks // 2
    segs = home * ny
    rows = segs * triggers
    names = nz * ny * per_group
    pairs = per_group * triggers
    half = pairs // 2
    share = half // nx
    reach = nz // 2
    depth = 2 * PIECE
    pieces = blocks // depth
    burst = min(BURST, pieces)
    bins = blocks * LANES
    first = ((x * 2 + core) * ny + y) * bins
    bank_rows = blocks // BANK_PARTS
    seg_rows = blocks // SEG_PARTS
    up, down = lax.rem(z + 1, nz), lax.rem(z + nz - 1, nz)

    def remote(src, dst, send, recv, where):
        return pltpu.make_async_remote_copy(
            src_ref=src, dst_ref=dst, send_sem=send, recv_sem=recv, device_id=where, device_id_type=MESH
        )

    def other_y(shift):
        return lax.rem(y + shift, ny)

    for m in range(per_group):
        pltpu.make_async_copy(bank.at[m], stage_b.at[:, m], bank_load).start()
    for shift in list(range(1, ny)) + [0]:
        span = pl.ds(other_y(shift) * blocks, blocks)

        def load(s, carry, shift=shift, span=span):
            if shift:
                dst = stage_s.at[shift - 1, :, s]
            else:
                dst = seg_buf.at[:, y * home + s]
            pltpu.make_async_copy(strain.at[s, span], dst, seg_load.at[shift]).start()
            return carry

        lax.fori_loop(0, home, load, 0)

    barrier = pltpu.get_barrier_semaphore()
    plane = [(dx, dy) for dx in range(nx) for dy in range(ny) if dx or dy]
    tpl = [(dx, dc) for dx in range(nx) for dc in range(2) if dx or dc]

    def at_plane(dx, dy):
        return {"x": lax.rem(x + dx, nx), "y": lax.rem(y + dy, ny)}

    def at_tpl(dx, dc):
        return {"x": lax.rem(x + dx, nx), "core": lax.rem(core + dc, 2)}

    greeted = [at_plane(dx, dy) for dx, dy in plane]
    greeted += [at_tpl(dx, dc) for dx, dc in tpl if dc]
    greeted += [{"z": up}, {"z": down}]
    for who in greeted:
        pl.semaphore_signal(barrier, inc=1, device_id=who, device_id_type=MESH)

    cos_a, sin_a = turns(iota((CHUNK, WINDOW), 0), iota((CHUNK, WINDOW), 1))
    inner[0] = cos_a
    inner[1] = sin_a
    cos_b, sin_b = turns(first + CHUNK * iota((chunks, WINDOW), 0), iota((chunks, WINDOW), 1))
    outer[0] = cos_b
    outer[1] = sin_b
    wanted = iota((2 * segs, 2 * segs), 0)
    wanted = jnp.where(wanted < segs, 2 * wanted, 2 * (wanted - segs) + 1)
    perm[...] = jnp.where(wanted == iota((2 * segs, 2 * segs), 1), 1.0, 0.0).astype(jnp.bfloat16)
    meta_buf[y] = meta[...]

    pltpu.make_async_copy(stage_b, stage_b, bank_load).wait()
    own_bank = pltpu.make_async_copy(
        stage_b.at[pl.ds(y * blocks, blocks)], bank_buf.at[:, z, pl.ds(y * per_group, per_group)], bank_own
    )
    own_bank.start()
    pl.semaphore_wait(barrier, len(greeted))

    def bank_part(part, shift):
        span = pl.ds(part * bank_rows, bank_rows)
        return remote(
            stage_b.at[pl.ds(other_y(shift) * blocks + part * bank_rows, bank_rows)],
            bank_buf.at[span, z, pl.ds(y * per_group, per_group)],
            yb_send.at[shift - 1], yb_recv.at[part, shift - 1], {"y": other_y(shift)},
        )

    def meta_part(shift):
        return remote(
            meta, meta_buf.at[y], meta_send.at[shift - 1], meta_recv.at[shift - 1], {"y": other_y(shift)}
        )

    def seg_part(part, shift):
        span = pl.ds(part * seg_rows, seg_rows)
        return remote(
            stage_s.at[shift - 1, span], seg_buf.at[span, pl.ds(y * home, home)],
            ys_send.at[shift - 1], ys_recv.at[part, shift - 1], {"y": other_y(shift)},
        )

    for shift in range(1, ny):
        bank_part(0, shift).start()
    for shift in range(1, ny):
        meta_part(shift).start()
    for part in range(1, BANK_PARTS):
        for shift in range(1, ny):
            bank_part(part, shift).start()
    for shift in range(1, ny):
        pltpu.make_async_copy(stage_s.at[shift - 1], stage_s.at[shift - 1], seg_load.at[shift]).wait()

    def send_segs(part, carry):
        for shift in range(1, ny):
            seg_part(part, shift).start()
        return carry

    lax.fori_loop(0, SEG_PARTS, send_segs, 0)
    own_bank.wait()

    def hop(chunk, h, rise):
        origin = lax.rem(z + (nz - h + 1 if rise else h - 1), nz)
        ref = bank_buf.at[pl.ds(depth * chunk, depth), origin]
        way = 0 if rise else 1
        return remote(
            ref, ref, z_send.at[way, h - 1], z_recv.at[way, h - 1, chunk], {"z": up if rise else down}
        )

    def landed(chunk, h, rise):
        origin = lax.rem(z + (nz - h if rise else h), nz)
        ref = bank_buf.at[pl.ds(depth * chunk, depth), origin]
        way = 0 if rise else 1
        remote(
            ref, ref, z_send.at[way, h - 1], z_recv.at[way, h - 1, chunk], {"z": up if rise else down}
        ).wait_recv()

    def when(cond, run):
        if isinstance(cond, bool):
            if cond:
                run()
        else:
            pl.when(cond)(run)

    def both(a, b):
        if isinstance(a, bool):
            return a and b
        return jnp.logical_and(a, b)

    def enter(chunk):
        per_part = bank_rows // depth

        def arrived():
            for shift in range(1, ny):
                bank_part(chunk // per_part, shift).wait_recv()

        when(chunk % per_part == 0, arrived)
        hop(chunk, 1, True).start()
        hop(chunk, 1, False).start()

    def tick(t):
        def last(chunk=t - LAG * reach):
            def go():
                when(chunk % 2 == 0, lambda: landed(chunk, reach, True))
                when(chunk % 2 == 1, lambda: landed(chunk, reach, False))

            when(both(chunk >= 0, chunk < pieces), go)

        last()
        for h in range(reach, 1, -1):
            chunk = t - LAG * (h - 1)

            def go(chunk=chunk, h=h):
                landed(chunk, h - 1, True)
                landed(chunk, h - 1, False)
                if h < reach:
                    hop(chunk, h, True).start()
                    hop(chunk, h, False).start()
                else:
                    when(chunk % 2 == 0, lambda: hop(chunk, h, True).start())
                    when(chunk % 2 == 1, lambda: hop(chunk, h, False).start())

            when(both(chunk >= 0, chunk < pieces), go)

        fresh = t + burst
        when(fresh < pieces, lambda: enter(fresh))

    def tables_phase(k):
        info = meta_buf[...].reshape(segs, LANES)
        off = info[:, 1 + k : 2 + k]
        cos_p, sin_p = turns(off, first + iota((segs, CHUNK), 1))
        phase[0, k * segs : (k + 1) * segs] = cos_p
        phase[1, k * segs : (k + 1) * segs] = sin_p
        cos_s, sin_s = turns(off, jnp.full((segs, LANES), CHUNK, jnp.int32))
        step[0, k * segs : (k + 1) * segs] = cos_s
        step[1, k * segs : (k + 1) * segs] = sin_s

    def tables_pick(k):
        info = meta_buf[...].reshape(segs, LANES)
        grp = info[:, 5 + k : 6 + k]
        spot = 2 * per_group * (lax.rem(grp, nz) * ny + lax.div(grp, nz))
        spot = jnp.broadcast_to(spot, (segs, 2 * names)) - iota((segs, 2 * names), 1)
        for m in range(per_group):
            to = slice((m * triggers + k) * segs, (m * triggers + k + 1) * segs)
            for part in range(2):
                hit = spot == -(2 * m + part)
                pick[part, to] = jnp.where(hit, 1.0, 0.0).astype(jnp.bfloat16)

    acc[...] = jnp.zeros_like(acc)
    norm[...] = jnp.zeros_like(norm)
    for c in range(burst):
        enter(c)
    ramp = LAG * reach
    for t in range(ramp):
        tick(t)
        if t == 0:
            for shift in range(1, ny):
                meta_part(shift).wait_recv()
        for k in range(triggers):
            if t == 1 + k * (ramp - 1) // triggers:
                tables_phase(k)
                tables_pick(k)
    pltpu.make_async_copy(
        seg_buf.at[:, pl.ds(y * home, home)], seg_buf.at[:, pl.ds(y * home, home)], seg_load.at[0]
    ).wait()

    def wait_segs(piece):
        per_part = seg_rows // depth

        def arrived():
            for shift in range(1, ny):
                seg_part(piece // per_part, shift).wait_recv()

        pl.when(piece % per_part == 0)(arrived)

    def filter_chunk(c):
        seg = jnp.concatenate([seg_buf[2 * c + i].reshape(2 * segs, LANES) for i in range(2)], axis=1)
        got = jnp.concatenate([bank_buf[2 * c + i].reshape(2 * names, LANES) for i in range(2)], axis=1)
        seg = jnp.dot(perm[...], seg, preferred_element_type=jnp.float32)
        w = wgt[:, pl.ds(pl.multiple_of(y * bins + c * CHUNK, CHUNK), CHUNK)]
        det = meta_buf[...].reshape(segs, LANES)[:, 0:1]
        chosen = jnp.where(det == 0, w[0:1], jnp.where(det == 1, w[1:2], w[2:3]))
        seg_re = (seg[:segs] * chosen)[None]
        seg_im = (seg[segs:] * chosen)[None]
        cos_p = phase[0]
        sin_p = phase[1]
        cos_k = cos_p.reshape(triggers, segs, CHUNK)
        sin_k = sin_p.reshape(triggers, segs, CHUNK)
        sh_re = (seg_re * cos_k - seg_im * sin_k).astype(jnp.bfloat16).astype(jnp.float32).reshape(rows, CHUNK)
        sh_im = (seg_re * sin_k + seg_im * cos_k).astype(jnp.bfloat16).astype(jnp.float32).reshape(rows, CHUNK)
        cos_s = jnp.concatenate([step[0], step[0]], axis=1)
        sin_s = jnp.concatenate([step[1], step[1]], axis=1)
        phase[0] = cos_p * cos_s - sin_p * sin_s
        phase[1] = cos_p * sin_s + sin_p * cos_s

        cos_b = outer[0, pl.ds(c, 1)]
        sin_b = outer[1, pl.ds(c, 1)]
        cos_e = (inner[0] * cos_b - inner[1] * sin_b).astype(jnp.bfloat16)
        sin_e = (inner[1] * cos_b + inner[0] * sin_b).astype(jnp.bfloat16)
        upper = jnp.concatenate([cos_e, sin_e], axis=1)
        lower = jnp.concatenate([-sin_e, cos_e], axis=1)
        for m in range(per_group):
            span = slice(m * rows, (m + 1) * rows)
            got_re = jnp.dot(pick[0, span], got, preferred_element_type=jnp.float32)
            got_im = jnp.dot(pick[1, span], got, preferred_element_type=jnp.float32)
            prod_re = (sh_re * got_re + sh_im * got_im).astype(jnp.bfloat16)
            prod_im = (sh_im * got_re - sh_re * got_im).astype(jnp.bfloat16)
            term = jnp.dot(prod_re, upper, preferred_element_type=jnp.float32)
            term = term + jnp.dot(prod_im, lower, preferred_element_type=jnp.float32)
            acc[m * triggers : (m + 1) * triggers] += term.reshape(triggers, segs, 2 * WINDOW)
        power = got.astype(jnp.float32)
        power = power * power
        for d in range(norm.shape[0]):
            scaled = power * (w[d : d + 1] * w[d : d + 1])
            norm[d] += scaled[:, :LANES] + scaled[:, LANES:]

    def advance(t, carry):
        tick(t)
        wait_segs(t - ramp)
        for i in range(PIECE):
            filter_chunk(PIECE * (t - ramp) + i)
        return carry

    lax.fori_loop(ramp, pieces + ramp, advance, 0)

    def core_part(dx):
        spot = lax.rem(x + dx, nx) * share
        return remote(
            acc.at[pl.ds((1 - core) * half + spot, share)], r0.at[pl.ds(spot, share)],
            r0_send.at[dx], r0_recv.at[dx], {"core": 1 - core},
        )

    def plane_part(i, dx, dy):
        who = at_plane(dx, dy)
        return remote(
            acc.at[pl.ds(core * half + who["x"] * share, share), pl.ds(who["y"] * home, home)],
            r1.at[i], r1_send.at[0, i], r1_recv.at[0, i], who,
        )

    def plane_norm(i, dx, dy):
        return remote(nsum, n1.at[i], r1_send.at[1, i], r1_recv.at[1, i], at_plane(dx, dy))

    far_first = sorted(range(nx), key=lambda dx: -min(dx, nx - dx))
    for dx in far_first:
        core_part(dx).start()
    ones = jnp.ones((8, LANES), jnp.float32)
    for d in range(norm.shape[0]):
        line = lax.dot_general(
            ones, norm[d], (((1,), (1,)), ((), ())),
            precision=lax.Precision.HIGHEST, preferred_element_type=jnp.float32,
        )
        nsum[d : d + 1] = line[0:1]
    nsum[norm.shape[0] :] = jnp.zeros((8 - norm.shape[0], 2 * names), jnp.float32)
    core_norm = remote(nsum, n0, r0_send.at[nx], r0_recv.at[nx], {"core": 1 - core})
    core_norm.start()
    for dx in far_first:
        core_part(dx).wait_recv()
        spot = lax.rem(x + dx, nx) * share
        mine = pl.ds(core * half + spot, share)
        acc[mine] = acc[mine] + r0[pl.ds(spot, share)]
        for i, (px, py) in enumerate(plane):
            if px == dx:
                plane_part(i, px, py).start()
    core_norm.wait()
    nsum[...] = nsum[...] + n0[...]
    for i, (dx, dy) in enumerate(plane):
        plane_norm(i, dx, dy).start()
    own = pl.ds(core * half + x * share, share)
    total = acc[own, pl.ds(pl.multiple_of(y * home, home), home)]
    for i, (dx, dy) in enumerate(plane):
        plane_part(i, dx, dy).wait_recv()
        total = total + r1[i]
    mags[own] = jnp.sqrt(total[:, :, :WINDOW] ** 2 + total[:, :, WINDOW:] ** 2)

    def tpl_part(i, dx, dc):
        return remote(mags.at[own], mags.at[own], r2_send.at[i], r2_recv.at[i], at_tpl(dx, dc))

    def tpl_landed(i, dx, dc):
        spot = lax.rem(core + dc, 2) * half + lax.rem(x + nx - dx, nx) * share
        ref = mags.at[pl.ds(spot, share)]
        remote(ref, ref, r2_send.at[i], r2_recv.at[i], at_tpl(dx, dc)).wait_recv()

    for i, (dx, dc) in enumerate(tpl):
        tpl_part(i, dx, dc).start()
    table = nsum[...]
    for i, (dx, dy) in enumerate(plane):
        plane_norm(i, dx, dy).wait_recv()
        table = table + n1[i]
    info = meta[...]
    det = info[:, 0:1]
    chosen = jnp.where(det == 0, table[0:1], jnp.where(det == 1, table[1:2], table[2:3]))
    place = lax.shift_right_logical(iota((home, 2 * names), 1), 1)
    roots = {}
    for k in range(triggers):
        grp = info[:, 5 + k : 6 + k]
        spot = per_group * (lax.rem(grp, nz) * ny + lax.div(grp, nz))
        for m in range(per_group):
            value = jnp.sum(jnp.where(place == spot + m, chosen, 0.0), axis=1, keepdims=True)
            roots[m * triggers + k] = jnp.sqrt(value + EPSILON)
    for i, (dx, dc) in enumerate(tpl):
        tpl_landed(i, dx, dc)
    for pair in range(pairs):
        level = mags[pair]
        snr[pair] = level / roots[pair]
        peak[pair] = jnp.max(level, axis=1, keepdims=True) / roots[pair]

    for shift in range(1, ny):
        remote(stage_b.at[pl.ds(0, blocks)], stage_b.at[pl.ds(0, blocks)], yb_send.at[shift - 1],
               yb_recv.at[0, shift - 1], {"y": other_y(shift)}).wait_send()
        meta_part(shift).wait_send()
        remote(stage_s.at[shift - 1], stage_s.at[shift - 1], ys_send.at[shift - 1],
               ys_recv.at[0, shift - 1], {"y": other_y(shift)}).wait_send()
    for way in range(2):
        for h in range(1, reach + 1):
            ref = bank_buf.at[:, 0] if h < reach else bank_buf.at[pl.ds(0, blocks // 2), 0]
            remote(ref, ref, z_send.at[way, h - 1], z_recv.at[way, h - 1, 0], {"z": up}).wait_send()
    for dx in far_first:
        core_part(dx).wait_send()
    for i, (dx, dy) in enumerate(plane):
        plane_part(i, dx, dy).wait_send()
        plane_norm(i, dx, dy).wait_send()
    for i, (dx, dc) in enumerate(tpl):
        tpl_part(i, dx, dc).wait_send()


def filter_bins(dims, strain, bank, meta, wgt):
    nx, ny, nz = dims
    home, whole_blocks = strain.shape[0], strain.shape[1]
    per_group = bank.shape[0]
    blocks = whole_blocks // ny
    chunks = blocks // 2
    segs, triggers = home * ny, 4
    rows = segs * triggers
    names = nz * ny * per_group
    pairs = per_group * triggers
    half = pairs // 2
    share = half // nx
    near = nx * ny - 1
    reach = nz // 2
    dets = wgt.shape[0]
    f32, bf16 = jnp.float32, jnp.bfloat16
    dma = pltpu.SemaphoreType.DMA
    total = rows * per_group
    any_space = pl.BlockSpec(memory_space=pl.ANY)
    vmem = pl.BlockSpec(memory_space=pltpu.VMEM)
    return pl.pallas_call(
        functools.partial(filter_kernel, dims),
        in_specs=[any_space, any_space, vmem, vmem],
        out_specs=[vmem, vmem],
        out_shape=[
            jax.ShapeDtypeStruct((pairs, home, WINDOW), f32),
            jax.ShapeDtypeStruct((pairs, home, 1), f32),
        ],
        scratch_shapes=[
            pltpu.VMEM((whole_blocks, per_group, 2, LANES), bf16),
            pltpu.VMEM((ny - 1, blocks, home, 2, LANES), bf16),
            pltpu.VMEM((blocks, nz, ny * per_group, 2, LANES), bf16),
            pltpu.VMEM((blocks, segs, 2, LANES), bf16),
            pltpu.VMEM((ny, home, LANES), jnp.int32),
            pltpu.VMEM((2, total, 2 * names), bf16),
            pltpu.VMEM((2 * segs, 2 * segs), bf16),
            pltpu.VMEM((2, rows, CHUNK), f32),
            pltpu.VMEM((2, rows, LANES), f32),
            pltpu.VMEM((2, CHUNK, WINDOW), f32),
            pltpu.VMEM((2, chunks, WINDOW), f32),
            pltpu.VMEM((pairs, segs, 2 * WINDOW), f32),
            pltpu.VMEM((dets, 2 * names, LANES), f32),
            pltpu.VMEM((8, 2 * names), f32),
            pltpu.VMEM((half, segs, 2 * WINDOW), f32),
            pltpu.VMEM((8, 2 * names), f32),
            pltpu.VMEM((near, share, home, 2 * WINDOW), f32),
            pltpu.VMEM((near, 8, 2 * names), f32),
            pltpu.VMEM((pairs, home, WINDOW), f32),
            dma, dma, dma((ny,)),
            dma((ny - 1,)), dma((BANK_PARTS, ny - 1)),
            dma((ny - 1,)), dma((SEG_PARTS, ny - 1)),
            dma((ny - 1,)), dma((ny - 1,)),
            dma((2, reach)), dma((2, reach, chunks // PIECE)),
            dma((nx + 1,)), dma((nx + 1,)),
            dma((2, near)), dma((2, near)),
            dma((2 * nx - 1,)), dma((2 * nx - 1,)),
        ],
        compiler_params=pltpu.CompilerParams(
            collective_id=0, has_side_effects=True, vmem_limit_bytes=56 * 1024 * 1024
        ),
        cost_estimate=pl.CostEstimate(
            flops=2 * total * blocks * LANES * 1024, bytes_accessed=4 << 20, transcendentals=0
        ),
    )(strain, bank, meta, wgt)


def body(dims, strain, templates, weights, detectors, offsets, routes):
    nx = dims[0]
    home, triggers = routes.shape

    def by_blocks(a):
        return a.reshape(a.shape[0], 2, -1, LANES).transpose(0, 2, 1, 3)

    meta = jnp.concatenate([detectors[:, None], offsets, routes], axis=1)
    meta = jnp.pad(meta, ((0, 0), (0, LANES - meta.shape[1])))
    snr, peak = filter_bins(dims, by_blocks(strain), by_blocks(templates), meta, weights)
    width = WINDOW // (2 * nx)
    at = lax.axis_index("x") * 2 + lax.axis_index("core")
    snr = lax.dynamic_slice_in_dim(snr, at * width, width, 2)
    snr = snr.reshape(-1, triggers, home, width).transpose(2, 1, 0, 3)
    peak = peak.reshape(-1, triggers, home).transpose(2, 1, 0)
    return snr, peak


def solution(mesh):
    devices = mesh.devices
    ny = 4 if devices.shape[0] % 4 == 0 and devices.shape[0] > 8 else 2
    nz = devices.shape[0] // ny
    nx = devices.shape[1] // 2
    fine = Mesh(devices.reshape(ny, nz, nx, 2), ("y", "z", "x", "core"))
    grp, tpl = ("y", "z"), ("x", "core")
    return jax.shard_map(
        functools.partial(body, (nx, ny, nz)),
        mesh=fine,
        in_specs=(
            P(grp, None, tpl),
            P(grp, None, tpl),
            P(None, tpl),
            P(grp),
            P(grp, None),
            P(grp, None),
        ),
        out_specs=(P(grp, None, None, tpl), P(grp, None, None)),
        check_vma=False,
    )
```

```python
import functools
import math

import jax
import jax.numpy as jnp
from jax import lax
from jax.experimental import pallas as pl
from jax.experimental.pallas import tpu as pltpu
from jax.sharding import Mesh
from jax.sharding import PartitionSpec as P

SAMPLES = 1048576
WINDOW = 128
LANES = 128
CHUNK = 2 * LANES
PIECE = 2
LAG = 2
BURST = 4
BANK_PARTS = 4
SEG_PARTS = 8
TWO_PI = 2.0 * math.pi
EPSILON = 1e-06
MESH = pl.DeviceIdType.MESH


def turns(index, moment):
    angles = ((index * moment) & (SAMPLES - 1)).astype(jnp.float32) * (TWO_PI / SAMPLES)
    return jnp.cos(angles), jnp.sin(angles)


def iota(shape, dim):
    return lax.broadcasted_iota(jnp.int32, shape, dim)


def filter_kernel(
    dims, strain, bank, dets, offs, names_in, wgt, snr, peak,
    stage_b, stage_s, bank_buf, seg_buf, meta, meta_buf, pick, perm, phase, step, inner, outer,
    acc, thin, norm, nsum, n0, r1, n1, mags,
    bank_load, bank_own, seg_load, yb_send, yb_recv, ys_send, ys_recv, meta_send, meta_recv,
    z_send, z_recv, n0_send, n0_recv, n1_send, n1_recv, r1_send, r1_recv, r2_send, r2_recv,
):
    nx, ny, nz = dims
    x, y, z, core = (lax.axis_index(a) for a in ("x", "y", "z", "core"))
    home, triggers = strain.shape[0], 4
    per_group = bank.shape[0]
    blocks = bank_buf.shape[0]
    chunks = blocks // 2
    segs = home * ny
    rows = segs * triggers
    names = nz * ny * per_group
    pairs = per_group * triggers
    share = pairs // (2 * nx)
    reach = nz // 2
    depth = 2 * PIECE
    pieces = blocks // depth
    burst = min(BURST, pieces)
    bins = blocks * LANES
    first = ((x * 2 + core) * ny + y) * bins
    bank_rows = blocks // BANK_PARTS
    seg_rows = blocks // SEG_PARTS
    up, down = lax.rem(z + 1, nz), lax.rem(z + nz - 1, nz)

    def remote(src, dst, send, recv, where):
        return pltpu.make_async_remote_copy(
            src_ref=src, dst_ref=dst, send_sem=send, recv_sem=recv, device_id=where, device_id_type=MESH
        )

    def other_y(shift):
        return lax.rem(y + shift, ny)

    barrier = pltpu.get_barrier_semaphore()

    def ring(i, n):
        return min(i, n - i)

    level = [(dx, dy, dc) for dx in range(nx) for dy in range(ny) for dc in range(2) if dx or dy or dc]
    level.sort(key=lambda d: -(ring(d[0], nx) + ring(d[1], ny)))
    plane = [d[:2] for d in level if not d[2]]
    tpl = [(d[0], d[2]) for d in level if not d[1]]

    def at_level(dx, dy, dc):
        return {"x": lax.rem(x + dx, nx), "y": lax.rem(y + dy, ny), "core": lax.rem(core + dc, 2)}

    greeted = [at_level(*d) for d in level] + [{"z": up}, {"z": down}]
    for who in greeted:
        pl.semaphore_signal(barrier, inc=1, device_id=who, device_id_type=MESH)

    for m in range(per_group):
        pltpu.make_async_copy(bank.at[m], stage_b.at[:, m], bank_load).start()
    for shift in list(range(1, ny)) + [0]:
        span = pl.ds(other_y(shift) * blocks, blocks)

        def load(s, carry, shift=shift, span=span):
            if shift:
                dst = stage_s.at[shift - 1, :, s]
            else:
                dst = seg_buf.at[:, y * home + s]
            pltpu.make_async_copy(strain.at[s, span], dst, seg_load.at[shift]).start()
            return carry

        lax.fori_loop(0, home, load, 0)

    square = (home, home)
    lines = [dets[...]] + [r[k : k + 1] for r in (offs, names_in) for k in range(triggers)]
    meta[...] = jnp.zeros_like(meta)
    for at, line in enumerate(lines):
        across = jnp.broadcast_to(line.astype(jnp.float32), square)
        across = jnp.where(iota(square, 0) == iota(square, 1), across, 0.0)
        meta[:, at : at + 1] = jnp.sum(across, axis=1, keepdims=True).astype(jnp.int32)
    meta_buf[y] = meta[...]

    pltpu.make_async_copy(stage_b, stage_b, bank_load).wait()
    own_bank = pltpu.make_async_copy(
        stage_b.at[pl.ds(y * blocks, blocks)], bank_buf.at[:, z, pl.ds(y * per_group, per_group)], bank_own
    )
    own_bank.start()
    pl.semaphore_wait(barrier, len(greeted))

    def bank_part(part, shift):
        span = pl.ds(part * bank_rows, bank_rows)
        return remote(
            stage_b.at[pl.ds(other_y(shift) * blocks + part * bank_rows, bank_rows)],
            bank_buf.at[span, z, pl.ds(y * per_group, per_group)],
            yb_send.at[shift - 1], yb_recv.at[part, shift - 1], {"y": other_y(shift)},
        )

    def meta_part(shift):
        return remote(
            meta, meta_buf.at[y], meta_send.at[shift - 1], meta_recv.at[shift - 1], {"y": other_y(shift)}
        )

    def seg_part(part, shift):
        span = pl.ds(part * seg_rows, seg_rows)
        return remote(
            stage_s.at[shift - 1, span], seg_buf.at[span, pl.ds(y * home, home)],
            ys_send.at[shift - 1], ys_recv.at[part, shift - 1], {"y": other_y(shift)},
        )

    for shift in range(1, ny):
        bank_part(0, shift).start()
    for shift in range(1, ny):
        meta_part(shift).start()
    for part in range(1, BANK_PARTS):
        for shift in range(1, ny):
            bank_part(part, shift).start()
    cos_a, sin_a = turns(iota((CHUNK, WINDOW), 0), iota((CHUNK, WINDOW), 1))
    inner[0] = cos_a
    inner[1] = sin_a
    cos_b, sin_b = turns(first + CHUNK * iota((chunks, WINDOW), 0), iota((chunks, WINDOW), 1))
    outer[0] = cos_b
    outer[1] = sin_b
    wanted = iota((2 * segs, 2 * segs), 0)
    wanted = jnp.where(wanted < segs, 2 * wanted, 2 * (wanted - segs) + 1)
    perm[...] = jnp.where(wanted == iota((2 * segs, 2 * segs), 1), 1.0, 0.0).astype(jnp.bfloat16)
    acc[...] = jnp.zeros_like(acc)
    norm[...] = jnp.zeros_like(norm)
    own_bank.wait()

    def hop(chunk, h, rise):
        origin = lax.rem(z + (nz - h + 1 if rise else h - 1), nz)
        ref = bank_buf.at[pl.ds(depth * chunk, depth), origin]
        way = 0 if rise else 1
        return remote(
            ref, ref, z_send.at[way, h - 1], z_recv.at[way, h - 1, chunk], {"z": up if rise else down}
        )

    def landed(chunk, h, rise):
        origin = lax.rem(z + (nz - h if rise else h), nz)
        ref = bank_buf.at[pl.ds(depth * chunk, depth), origin]
        way = 0 if rise else 1
        remote(
            ref, ref, z_send.at[way, h - 1], z_recv.at[way, h - 1, chunk], {"z": up if rise else down}
        ).wait_recv()

    def when(cond, run):
        if isinstance(cond, bool):
            if cond:
                run()
        else:
            pl.when(cond)(run)

    def both(a, b):
        if isinstance(a, bool):
            return a and b
        return jnp.logical_and(a, b)

    def enter(chunk):
        per_part = bank_rows // depth

        def arrived():
            for shift in range(1, ny):
                bank_part(chunk // per_part, shift).wait_recv()

        when(chunk % per_part == 0, arrived)
        hop(chunk, 1, True).start()
        hop(chunk, 1, False).start()

    def tick(t):
        def last(chunk=t - LAG * reach):
            def go():
                when(chunk % 2 == 0, lambda: landed(chunk, reach, True))
                when(chunk % 2 == 1, lambda: landed(chunk, reach, False))

            when(both(chunk >= 0, chunk < pieces), go)

        last()
        for h in range(reach, 1, -1):
            chunk = t - LAG * (h - 1)

            def go(chunk=chunk, h=h):
                landed(chunk, h - 1, True)
                landed(chunk, h - 1, False)
                if h < reach:
                    hop(chunk, h, True).start()
                    hop(chunk, h, False).start()
                else:
                    when(chunk % 2 == 0, lambda: hop(chunk, h, True).start())
                    when(chunk % 2 == 1, lambda: hop(chunk, h, False).start())

            when(both(chunk >= 0, chunk < pieces), go)

        fresh = t + burst
        when(fresh < pieces, lambda: enter(fresh))

    def tables_phase(k):
        info = meta_buf[...].reshape(segs, LANES)
        off = info[:, 1 + k : 2 + k]
        cos_p, sin_p = turns(off, first + iota((segs, CHUNK), 1))
        phase[0, k * segs : (k + 1) * segs] = cos_p
        phase[1, k * segs : (k + 1) * segs] = sin_p
        cos_s, sin_s = turns(off, jnp.full((segs, LANES), CHUNK, jnp.int32))
        step[0, k * segs : (k + 1) * segs] = cos_s
        step[1, k * segs : (k + 1) * segs] = sin_s

    def tables_pick(k):
        info = meta_buf[...].reshape(segs, LANES)
        grp = info[:, 5 + k : 6 + k]
        spot = 2 * per_group * (lax.rem(grp, nz) * ny + lax.div(grp, nz))
        spot = jnp.broadcast_to(spot, (segs, 2 * names)) - iota((segs, 2 * names), 1)
        for m in range(per_group):
            to = slice((m * triggers + k) * segs, (m * triggers + k + 1) * segs)
            for part in range(2):
                hit = spot == -(2 * m + part)
                pick[part, to] = jnp.where(hit, 1.0, 0.0).astype(jnp.bfloat16)

    for c in range(burst):
        enter(c)
    for shift in range(1, ny):
        pltpu.make_async_copy(stage_s.at[shift - 1], stage_s.at[shift - 1], seg_load.at[shift]).wait()

    def send_segs(part, carry):
        for shift in range(1, ny):
            seg_part(part, shift).start()
        return carry

    lax.fori_loop(0, SEG_PARTS, send_segs, 0)
    ramp = LAG * reach
    for t in range(ramp):
        tick(t)
        if t == 0:
            for shift in range(1, ny):
                meta_part(shift).wait_recv()
        for k in range(triggers):
            if t == 1 + k * (ramp - 1) // triggers:
                tables_phase(k)
                tables_pick(k)
    pltpu.make_async_copy(
        seg_buf.at[:, pl.ds(y * home, home)], seg_buf.at[:, pl.ds(y * home, home)], seg_load.at[0]
    ).wait()

    def wait_segs(piece):
        per_part = seg_rows // depth

        def arrived():
            for shift in range(1, ny):
                seg_part(piece // per_part, shift).wait_recv()

        pl.when(piece % per_part == 0)(arrived)

    def filter_chunk(c):
        seg = jnp.concatenate([seg_buf[2 * c + i].reshape(2 * segs, LANES) for i in range(2)], axis=1)
        got = jnp.concatenate([bank_buf[2 * c + i].reshape(2 * names, LANES) for i in range(2)], axis=1)
        seg = jnp.dot(perm[...], seg, preferred_element_type=jnp.float32)
        w = wgt[:, pl.ds(pl.multiple_of(y * bins + c * CHUNK, CHUNK), CHUNK)]
        det = meta_buf[...].reshape(segs, LANES)[:, 0:1]
        chosen = jnp.where(det == 0, w[0:1], jnp.where(det == 1, w[1:2], w[2:3]))
        seg_re = (seg[:segs] * chosen)[None]
        seg_im = (seg[segs:] * chosen)[None]
        cos_p = phase[0]
        sin_p = phase[1]
        cos_k = cos_p.reshape(triggers, segs, CHUNK)
        sin_k = sin_p.reshape(triggers, segs, CHUNK)
        sh_re = (seg_re * cos_k - seg_im * sin_k).astype(jnp.bfloat16).astype(jnp.float32).reshape(rows, CHUNK)
        sh_im = (seg_re * sin_k + seg_im * cos_k).astype(jnp.bfloat16).astype(jnp.float32).reshape(rows, CHUNK)
        cos_s = jnp.concatenate([step[0], step[0]], axis=1)
        sin_s = jnp.concatenate([step[1], step[1]], axis=1)
        phase[0] = cos_p * cos_s - sin_p * sin_s
        phase[1] = cos_p * sin_s + sin_p * cos_s

        cos_b = outer[0, pl.ds(c, 1)]
        sin_b = outer[1, pl.ds(c, 1)]
        cos_e = (inner[0] * cos_b - inner[1] * sin_b).astype(jnp.bfloat16)
        sin_e = (inner[1] * cos_b + inner[0] * sin_b).astype(jnp.bfloat16)
        upper = jnp.concatenate([cos_e, sin_e], axis=1)
        lower = jnp.concatenate([-sin_e, cos_e], axis=1)
        for m in range(per_group):
            span = slice(m * rows, (m + 1) * rows)
            got_re = jnp.dot(pick[0, span], got, preferred_element_type=jnp.float32)
            got_im = jnp.dot(pick[1, span], got, preferred_element_type=jnp.float32)
            prod_re = (sh_re * got_re + sh_im * got_im).astype(jnp.bfloat16)
            prod_im = (sh_im * got_re - sh_re * got_im).astype(jnp.bfloat16)
            term = jnp.dot(prod_re, upper, preferred_element_type=jnp.float32)
            term = term + jnp.dot(prod_im, lower, preferred_element_type=jnp.float32)
            acc[m * triggers : (m + 1) * triggers] += term.reshape(triggers, segs, 2 * WINDOW)
        power = got.astype(jnp.float32)
        power = power * power
        for d in range(norm.shape[0]):
            scaled = power * (w[d : d + 1] * w[d : d + 1])
            norm[d] += scaled[:, :LANES] + scaled[:, LANES:]

    def advance(t, carry):
        tick(t)
        wait_segs(t - ramp)
        for i in range(PIECE):
            filter_chunk(PIECE * (t - ramp) + i)
        return carry

    lax.fori_loop(ramp, pieces + ramp, advance, 0)

    def level_part(i):
        who = at_level(*level[i])
        return remote(
            thin.at[pl.ds((who["core"] * nx + who["x"]) * share, share), pl.ds(who["y"] * home, home)],
            r1.at[i], r1_send.at[i], r1_recv.at[i], who,
        )

    def plane_norm(i, dx, dy):
        return remote(nsum, n1.at[i], n1_send.at[i], n1_recv.at[i], at_level(dx, dy, 0))

    thin[...] = acc[...].astype(jnp.bfloat16)
    for i in range(len(level)):
        level_part(i).start()
    ones = jnp.ones((8, LANES), jnp.float32)
    halves = jnp.where(
        lax.shift_right_logical(iota((2 * names, names), 0), 1) == iota((2 * names, names), 1), 1.0, 0.0
    )
    nsum[...] = jnp.zeros_like(nsum)
    for d in range(norm.shape[0]):
        line = lax.dot_general(
            ones, norm[d], (((1,), (1,)), ((), ())),
            precision=lax.Precision.HIGHEST, preferred_element_type=jnp.float32,
        )
        line = jnp.dot(line, halves, precision=lax.Precision.HIGHEST, preferred_element_type=jnp.float32)
        nsum[d : d + 1] = line[0:1]
    core_norm = remote(nsum, n0, n0_send, n0_recv, {"core": 1 - core})
    core_norm.start()
    core_norm.wait()
    nsum[...] = nsum[...] + n0[...]
    for i, (dx, dy) in enumerate(plane):
        plane_norm(i, dx, dy).start()
    own = pl.ds((core * nx + x) * share, share)
    total = acc[own, pl.ds(pl.multiple_of(y * home, home), home)]
    for i in range(len(level)):
        level_part(i).wait_recv()
        total = total + r1[i].astype(jnp.float32)
    mags[own] = jnp.sqrt(total[:, :, :WINDOW] ** 2 + total[:, :, WINDOW:] ** 2)

    def tpl_part(i, dx, dc):
        return remote(mags.at[own], mags.at[own], r2_send.at[i], r2_recv.at[i], at_level(dx, 0, dc))

    def tpl_landed(i, dx, dc):
        spot = (lax.rem(core + dc, 2) * nx + lax.rem(x + nx - dx, nx)) * share
        ref = mags.at[pl.ds(spot, share)]
        remote(ref, ref, r2_send.at[i], r2_recv.at[i], at_level(dx, 0, dc)).wait_recv()

    for i, (dx, dc) in enumerate(tpl):
        tpl_part(i, dx, dc).start()
    table = nsum[...]
    for i, (dx, dy) in enumerate(plane):
        plane_norm(i, dx, dy).wait_recv()
        table = table + n1[i]
    info = meta[...]
    det = info[:, 0:1]
    chosen = jnp.where(det == 0, table[0:1], jnp.where(det == 1, table[1:2], table[2:3]))
    place = iota((home, names), 1)
    roots = {}
    for k in range(triggers):
        grp = info[:, 5 + k : 6 + k]
        spot = per_group * (lax.rem(grp, nz) * ny + lax.div(grp, nz))
        for m in range(per_group):
            value = jnp.sum(jnp.where(place == spot + m, chosen, 0.0), axis=1, keepdims=True)
            roots[m * triggers + k] = jnp.sqrt(value + EPSILON)
    for i, (dx, dc) in enumerate(tpl):
        tpl_landed(i, dx, dc)
    width = snr.shape[-1]
    turn = lax.rem(WINDOW - (x * 2 + core) * width, WINDOW)
    tops = jnp.zeros((home, pairs), jnp.float32)
    for k in range(triggers):
        for m in range(per_group):
            ratio = mags[m * triggers + k] / roots[m * triggers + k]
            top = jnp.max(mags[m * triggers + k], axis=1, keepdims=True) / roots[m * triggers + k]
            snr[:, k, m, :] = pltpu.roll(ratio, turn, 1)[:, :width]
            tops = jnp.where(iota((home, pairs), 1) == k * per_group + m, top, tops)
    peak[...] = tops

    for shift in range(1, ny):
        remote(stage_b.at[pl.ds(0, blocks)], stage_b.at[pl.ds(0, blocks)], yb_send.at[shift - 1],
               yb_recv.at[0, shift - 1], {"y": other_y(shift)}).wait_send()
        meta_part(shift).wait_send()
        remote(stage_s.at[shift - 1], stage_s.at[shift - 1], ys_send.at[shift - 1],
               ys_recv.at[0, shift - 1], {"y": other_y(shift)}).wait_send()
    for way in range(2):
        for h in range(1, reach + 1):
            ref = bank_buf.at[:, 0] if h < reach else bank_buf.at[pl.ds(0, blocks // 2), 0]
            remote(ref, ref, z_send.at[way, h - 1], z_recv.at[way, h - 1, 0], {"z": up}).wait_send()
    for i in range(len(level)):
        level_part(i).wait_send()
    for i, (dx, dy) in enumerate(plane):
        plane_norm(i, dx, dy).wait_send()
    for i, (dx, dc) in enumerate(tpl):
        tpl_part(i, dx, dc).wait_send()


def filter_bins(dims, strain, bank, dets, offs, names_in, wgt):
    nx, ny, nz = dims
    home, whole_blocks = strain.shape[0], strain.shape[1]
    per_group = bank.shape[0]
    blocks = whole_blocks // ny
    chunks = blocks // 2
    segs, triggers = home * ny, 4
    rows = segs * triggers
    names = nz * ny * per_group
    pairs = per_group * triggers
    share = pairs // (2 * nx)
    near = nx * ny - 1
    level = 2 * nx * ny - 1
    reach = nz // 2
    width = WINDOW // (2 * nx)
    f32, bf16 = jnp.float32, jnp.bfloat16
    dma = pltpu.SemaphoreType.DMA
    total = rows * per_group
    any_space = pl.BlockSpec(memory_space=pl.ANY)
    vmem = pl.BlockSpec(memory_space=pltpu.VMEM)
    return pl.pallas_call(
        functools.partial(filter_kernel, dims),
        in_specs=[any_space, any_space, vmem, vmem, vmem, vmem],
        out_specs=[vmem, vmem],
        out_shape=[
            jax.ShapeDtypeStruct((home, triggers, per_group, width), f32),
            jax.ShapeDtypeStruct((home, pairs), f32),
        ],
        scratch_shapes=[
            pltpu.VMEM((whole_blocks, per_group, 2, LANES), bf16),
            pltpu.VMEM((ny - 1, blocks, home, 2, LANES), bf16),
            pltpu.VMEM((blocks, nz, ny * per_group, 2, LANES), bf16),
            pltpu.VMEM((blocks, segs, 2, LANES), bf16),
            pltpu.VMEM((home, LANES), jnp.int32),
            pltpu.VMEM((ny, home, LANES), jnp.int32),
            pltpu.VMEM((2, total, 2 * names), bf16),
            pltpu.VMEM((2 * segs, 2 * segs), bf16),
            pltpu.VMEM((2, rows, CHUNK), f32),
            pltpu.VMEM((2, rows, LANES), f32),
            pltpu.VMEM((2, CHUNK, WINDOW), f32),
            pltpu.VMEM((2, chunks, WINDOW), f32),
            pltpu.VMEM((pairs, segs, 2 * WINDOW), f32),
            pltpu.VMEM((pairs, segs, 2 * WINDOW), bf16),
            pltpu.VMEM((wgt.shape[0], 2 * names, LANES), f32),
            pltpu.VMEM((8, names), f32),
            pltpu.VMEM((8, names), f32),
            pltpu.VMEM((level, share, home, 2 * WINDOW), bf16),
            pltpu.VMEM((near, 8, names), f32),
            pltpu.VMEM((pairs, home, WINDOW), f32),
            dma, dma, dma((ny,)),
            dma((ny - 1,)), dma((BANK_PARTS, ny - 1)),
            dma((ny - 1,)), dma((SEG_PARTS, ny - 1)),
            dma((ny - 1,)), dma((ny - 1,)),
            dma((2, reach)), dma((2, reach, chunks // PIECE)),
            dma, dma, dma((near,)), dma((near,)), dma((level,)), dma((level,)),
            dma((2 * nx - 1,)), dma((2 * nx - 1,)),
        ],
        compiler_params=pltpu.CompilerParams(
            collective_id=0, has_side_effects=True, vmem_limit_bytes=56 * 1024 * 1024
        ),
        cost_estimate=pl.CostEstimate(
            flops=2 * total * blocks * LANES * 1024, bytes_accessed=4 << 20, transcendentals=0
        ),
    )(strain, bank, dets, offs, names_in, wgt)


def body(dims, strain, templates, weights, detectors, offsets, routes):
    home, triggers = routes.shape

    def by_blocks(a):
        return a.reshape(a.shape[0], 2, -1, LANES).transpose(0, 2, 1, 3)

    snr, peak = filter_bins(
        dims, by_blocks(strain), by_blocks(templates), detectors[None, :], offsets.T, routes.T, weights
    )
    return snr, peak.reshape(home, triggers, -1)


def solution(mesh):
    devices = mesh.devices
    ny = 4 if devices.shape[0] % 4 == 0 and devices.shape[0] > 8 else 2
    nz = devices.shape[0] // ny
    nx = devices.shape[1] // 2
    fine = Mesh(devices.reshape(ny, nz, nx, 2), ("y", "z", "x", "core"))
    grp, tpl = ("y", "z"), ("x", "core")
    return jax.shard_map(
        functools.partial(body, (nx, ny, nz)),
        mesh=fine,
        in_specs=(
            P(grp, None, tpl),
            P(grp, None, tpl),
            P(None, tpl),
            P(grp),
            P(grp, None),
            P(grp, None),
        ),
        out_specs=(P(grp, None, None, tpl), P(grp, None, None)),
        check_vma=False,
    )
```

```python
import functools
import math

import jax
import jax.numpy as jnp
from jax import lax
from jax.experimental import pallas as pl
from jax.experimental.pallas import tpu as pltpu
from jax.sharding import Mesh
from jax.sharding import PartitionSpec as P

SAMPLES = 1048576
WINDOW = 128
LANES = 128
CHUNK = 2 * LANES
PIECE = 2
LAG = 2
BURST = 2
BANK_PARTS = 8
SEG_PARTS = 8
TWO_PI = 2.0 * math.pi
EPSILON = 1e-06
MESH = pl.DeviceIdType.MESH


def turns(index, moment):
    angles = ((index * moment) & (SAMPLES - 1)).astype(jnp.float32) * (TWO_PI / SAMPLES)
    return jnp.cos(angles), jnp.sin(angles)


def iota(shape, dim):
    return lax.broadcasted_iota(jnp.int32, shape, dim)


def filter_kernel(
    dims, strain, bank, dets, offs, names_in, wgt, snr, peak,
    stage_b, stage_s, bank_buf, seg_buf, meta, meta_buf, pick, perm, phase, step, inner, outer,
    acc, thin, norm, nsum, n0, r1, n1, mags,
    bank_load, bank_own, seg_load, yb_send, yb_recv, ys_send, ys_recv, meta_send, meta_recv,
    z_send, z_recv, n0_send, n0_recv, n1_send, n1_recv, r1_send, r1_recv, r2_send, r2_recv,
):
    nx, ny, nz = dims
    x, y, z, core = (lax.axis_index(a) for a in ("x", "y", "z", "core"))
    home, triggers = strain.shape[0], 4
    per_group = bank.shape[0]
    blocks = bank_buf.shape[0]
    chunks = blocks // 2
    segs = home * ny
    rows = segs * triggers
    names = nz * ny * per_group
    pairs = per_group * triggers
    share = pairs // (2 * nx)
    reach = nz // 2
    depth = 2 * PIECE
    pieces = blocks // depth
    burst = min(BURST, pieces)
    bins = blocks * LANES
    first = ((x * 2 + core) * ny + y) * bins
    bank_rows = blocks // BANK_PARTS
    seg_rows = blocks // SEG_PARTS
    up, down = lax.rem(z + 1, nz), lax.rem(z + nz - 1, nz)

    def remote(src, dst, send, recv, where):
        return pltpu.make_async_remote_copy(
            src_ref=src, dst_ref=dst, send_sem=send, recv_sem=recv, device_id=where, device_id_type=MESH
        )

    def other_y(shift):
        return lax.rem(y + shift, ny)

    barrier = pltpu.get_barrier_semaphore()

    def ring(i, n):
        return min(i, n - i)

    level = [(dx, dy, dc) for dx in range(nx) for dy in range(ny) for dc in range(2) if dx or dy or dc]
    level.sort(key=lambda d: -(ring(d[0], nx) + ring(d[1], ny)))
    plane = [d[:2] for d in level if not d[2]]
    tpl = [(d[0], d[2]) for d in level if not d[1]]

    def at_level(dx, dy, dc):
        return {"x": lax.rem(x + dx, nx), "y": lax.rem(y + dy, ny), "core": lax.rem(core + dc, 2)}

    greeted = [at_level(*d) for d in level] + [{"z": up}, {"z": down}]
    for who in greeted:
        pl.semaphore_signal(barrier, inc=1, device_id=who, device_id_type=MESH)

    for m in range(per_group):
        pltpu.make_async_copy(bank.at[m], stage_b.at[:, m], bank_load).start()
    for shift in list(range(1, ny)) + [0]:
        span = pl.ds(other_y(shift) * blocks, blocks)

        def load(s, carry, shift=shift, span=span):
            if shift:
                dst = stage_s.at[shift - 1, :, s]
            else:
                dst = seg_buf.at[:, y * home + s]
            pltpu.make_async_copy(strain.at[s, span], dst, seg_load.at[shift]).start()
            return carry

        lax.fori_loop(0, home, load, 0)

    square = (home, home)
    lines = [dets[...]] + [r[k : k + 1] for r in (offs, names_in) for k in range(triggers)]
    meta[...] = jnp.zeros_like(meta)
    for at, line in enumerate(lines):
        across = jnp.broadcast_to(line.astype(jnp.float32), square)
        across = jnp.where(iota(square, 0) == iota(square, 1), across, 0.0)
        meta[:, at : at + 1] = jnp.sum(across, axis=1, keepdims=True).astype(jnp.int32)
    meta_buf[y] = meta[...]

    pltpu.make_async_copy(stage_b, stage_b, bank_load).wait()
    own_bank = pltpu.make_async_copy(
        stage_b.at[pl.ds(y * blocks, blocks)], bank_buf.at[:, z, pl.ds(y * per_group, per_group)], bank_own
    )
    own_bank.start()
    pl.semaphore_wait(barrier, len(greeted))

    def bank_part(part, shift):
        span = pl.ds(part * bank_rows, bank_rows)
        return remote(
            stage_b.at[pl.ds(other_y(shift) * blocks + part * bank_rows, bank_rows)],
            bank_buf.at[span, z, pl.ds(y * per_group, per_group)],
            yb_send.at[shift - 1], yb_recv.at[part, shift - 1], {"y": other_y(shift)},
        )

    def meta_part(shift):
        return remote(
            meta, meta_buf.at[y], meta_send.at[shift - 1], meta_recv.at[shift - 1], {"y": other_y(shift)}
        )

    def seg_part(part, shift):
        span = pl.ds(part * seg_rows, seg_rows)
        return remote(
            stage_s.at[shift - 1, span], seg_buf.at[span, pl.ds(y * home, home)],
            ys_send.at[shift - 1], ys_recv.at[part, shift - 1], {"y": other_y(shift)},
        )

    for shift in range(1, ny):
        bank_part(0, shift).start()
    for shift in range(1, ny):
        meta_part(shift).start()
    for part in range(1, BANK_PARTS):
        for shift in range(1, ny):
            bank_part(part, shift).start()
    cos_a, sin_a = turns(iota((CHUNK, WINDOW), 0), iota((CHUNK, WINDOW), 1))
    inner[0] = cos_a
    inner[1] = sin_a
    cos_b, sin_b = turns(first + CHUNK * iota((chunks, WINDOW), 0), iota((chunks, WINDOW), 1))
    outer[0] = cos_b
    outer[1] = sin_b
    wanted = iota((2 * segs, 2 * segs), 0)
    wanted = jnp.where(wanted < segs, 2 * wanted, 2 * (wanted - segs) + 1)
    perm[...] = jnp.where(wanted == iota((2 * segs, 2 * segs), 1), 1.0, 0.0).astype(jnp.bfloat16)
    acc[...] = jnp.zeros_like(acc)
    norm[...] = jnp.zeros_like(norm)
    own_bank.wait()

    def hop(chunk, h, rise):
        origin = lax.rem(z + (nz - h + 1 if rise else h - 1), nz)
        ref = bank_buf.at[pl.ds(depth * chunk, depth), origin]
        way = 0 if rise else 1
        return remote(
            ref, ref, z_send.at[way, h - 1], z_recv.at[way, h - 1, chunk], {"z": up if rise else down}
        )

    def landed(chunk, h, rise):
        origin = lax.rem(z + (nz - h if rise else h), nz)
        ref = bank_buf.at[pl.ds(depth * chunk, depth), origin]
        way = 0 if rise else 1
        remote(
            ref, ref, z_send.at[way, h - 1], z_recv.at[way, h - 1, chunk], {"z": up if rise else down}
        ).wait_recv()

    def when(cond, run):
        if isinstance(cond, bool):
            if cond:
                run()
        else:
            pl.when(cond)(run)

    def both(a, b):
        if isinstance(a, bool):
            return a and b
        return jnp.logical_and(a, b)

    def enter(chunk):
        per_part = bank_rows // depth

        def arrived():
            for shift in range(1, ny):
                bank_part(chunk // per_part, shift).wait_recv()

        when(chunk % per_part == 0, arrived)
        hop(chunk, 1, True).start()
        hop(chunk, 1, False).start()

    def tick(t):
        def last(chunk=t - LAG * reach):
            def go():
                when(chunk % 2 == 0, lambda: landed(chunk, reach, True))
                when(chunk % 2 == 1, lambda: landed(chunk, reach, False))

            when(both(chunk >= 0, chunk < pieces), go)

        last()
        for h in range(reach, 1, -1):
            chunk = t - LAG * (h - 1)

            def go(chunk=chunk, h=h):
                landed(chunk, h - 1, True)
                landed(chunk, h - 1, False)
                if h < reach:
                    hop(chunk, h, True).start()
                    hop(chunk, h, False).start()
                else:
                    when(chunk % 2 == 0, lambda: hop(chunk, h, True).start())
                    when(chunk % 2 == 1, lambda: hop(chunk, h, False).start())

            when(both(chunk >= 0, chunk < pieces), go)

        fresh = t + burst
        when(fresh < pieces, lambda: enter(fresh))

    def tables_phase(k):
        info = meta_buf[...].reshape(segs, LANES)
        off = info[:, 1 + k : 2 + k]
        cos_p, sin_p = turns(off, first + iota((segs, CHUNK), 1))
        phase[0, k * segs : (k + 1) * segs] = cos_p
        phase[1, k * segs : (k + 1) * segs] = sin_p
        cos_s, sin_s = turns(off, jnp.full((segs, LANES), CHUNK, jnp.int32))
        step[0, k * segs : (k + 1) * segs] = cos_s
        step[1, k * segs : (k + 1) * segs] = sin_s

    def tables_pick(k):
        info = meta_buf[...].reshape(segs, LANES)
        grp = info[:, 5 + k : 6 + k]
        spot = 2 * per_group * (lax.rem(grp, nz) * ny + lax.div(grp, nz))
        spot = jnp.broadcast_to(spot, (segs, 2 * names)) - iota((segs, 2 * names), 1)
        for m in range(per_group):
            to = slice((m * triggers + k) * segs, (m * triggers + k + 1) * segs)
            for part in range(2):
                hit = spot == -(2 * m + part)
                pick[part, to] = jnp.where(hit, 1.0, 0.0).astype(jnp.bfloat16)

    for c in range(burst):
        enter(c)
    for shift in range(1, ny):
        pltpu.make_async_copy(stage_s.at[shift - 1], stage_s.at[shift - 1], seg_load.at[shift]).wait()

    def send_segs(part, carry):
        for shift in range(1, ny):
            seg_part(part, shift).start()
        return carry

    lax.fori_loop(0, SEG_PARTS, send_segs, 0)
    ramp = LAG * reach
    for t in range(ramp):
        tick(t)
        if t == 0:
            for shift in range(1, ny):
                meta_part(shift).wait_recv()
        for k in range(triggers):
            if t == 1 + k * (ramp - 1) // triggers:
                tables_phase(k)
                tables_pick(k)
    pltpu.make_async_copy(
        seg_buf.at[:, pl.ds(y * home, home)], seg_buf.at[:, pl.ds(y * home, home)], seg_load.at[0]
    ).wait()

    def wait_segs(piece):
        per_part = seg_rows // depth

        def arrived():
            for shift in range(1, ny):
                seg_part(piece // per_part, shift).wait_recv()

        pl.when(piece % per_part == 0)(arrived)

    def filter_chunk(c):
        seg = jnp.concatenate([seg_buf[2 * c + i].reshape(2 * segs, LANES) for i in range(2)], axis=1)
        got = jnp.concatenate([bank_buf[2 * c + i].reshape(2 * names, LANES) for i in range(2)], axis=1)
        seg = jnp.dot(perm[...], seg, preferred_element_type=jnp.float32)
        w = wgt[:, pl.ds(pl.multiple_of(y * bins + c * CHUNK, CHUNK), CHUNK)]
        det = meta_buf[...].reshape(segs, LANES)[:, 0:1]
        chosen = jnp.where(det == 0, w[0:1], jnp.where(det == 1, w[1:2], w[2:3]))
        seg_re = (seg[:segs] * chosen)[None]
        seg_im = (seg[segs:] * chosen)[None]
        cos_p = phase[0]
        sin_p = phase[1]
        cos_k = cos_p.reshape(triggers, segs, CHUNK)
        sin_k = sin_p.reshape(triggers, segs, CHUNK)
        sh_re = (seg_re * cos_k - seg_im * sin_k).astype(jnp.bfloat16).astype(jnp.float32).reshape(rows, CHUNK)
        sh_im = (seg_re * sin_k + seg_im * cos_k).astype(jnp.bfloat16).astype(jnp.float32).reshape(rows, CHUNK)
        cos_s = jnp.concatenate([step[0], step[0]], axis=1)
        sin_s = jnp.concatenate([step[1], step[1]], axis=1)
        phase[0] = cos_p * cos_s - sin_p * sin_s
        phase[1] = cos_p * sin_s + sin_p * cos_s

        cos_b = outer[0, pl.ds(c, 1)]
        sin_b = outer[1, pl.ds(c, 1)]
        cos_e = (inner[0] * cos_b - inner[1] * sin_b).astype(jnp.bfloat16)
        sin_e = (inner[1] * cos_b + inner[0] * sin_b).astype(jnp.bfloat16)
        upper = jnp.concatenate([cos_e, sin_e], axis=1)
        lower = jnp.concatenate([-sin_e, cos_e], axis=1)
        for m in range(per_group):
            span = slice(m * rows, (m + 1) * rows)
            got_re = jnp.dot(pick[0, span], got, preferred_element_type=jnp.float32)
            got_im = jnp.dot(pick[1, span], got, preferred_element_type=jnp.float32)
            prod_re = (sh_re * got_re + sh_im * got_im).astype(jnp.bfloat16)
            prod_im = (sh_im * got_re - sh_re * got_im).astype(jnp.bfloat16)
            term = jnp.dot(prod_re, upper, preferred_element_type=jnp.float32)
            term = term + jnp.dot(prod_im, lower, preferred_element_type=jnp.float32)
            acc[m * triggers : (m + 1) * triggers] += term.reshape(triggers, segs, 2 * WINDOW)
        power = got.astype(jnp.float32)
        power = power * power
        for d in range(norm.shape[0]):
            scaled = power * (w[d : d + 1] * w[d : d + 1])
            norm[d] += scaled[:, :LANES] + scaled[:, LANES:]

    def advance(t, carry):
        tick(t)
        wait_segs(t - ramp)
        for i in range(PIECE):
            filter_chunk(PIECE * (t - ramp) + i)
        return carry

    lax.fori_loop(ramp, pieces + ramp, advance, 0)

    def level_part(i):
        who = at_level(*level[i])
        return remote(
            thin.at[pl.ds((who["core"] * nx + who["x"]) * share, share), pl.ds(who["y"] * home, home)],
            r1.at[i], r1_send.at[i], r1_recv.at[i], who,
        )

    def plane_norm(i, dx, dy):
        return remote(nsum, n1.at[i], n1_send.at[i], n1_recv.at[i], at_level(dx, dy, 0))

    thin[...] = acc[...].astype(jnp.bfloat16)
    for i in range(len(level)):
        level_part(i).start()
    ones = jnp.ones((8, LANES), jnp.float32)
    halves = jnp.where(
        lax.shift_right_logical(iota((2 * names, names), 0), 1) == iota((2 * names, names), 1), 1.0, 0.0
    )
    nsum[...] = jnp.zeros_like(nsum)
    for d in range(norm.shape[0]):
        line = lax.dot_general(
            ones, norm[d], (((1,), (1,)), ((), ())),
            precision=lax.Precision.HIGHEST, preferred_element_type=jnp.float32,
        )
        line = jnp.dot(line, halves, precision=lax.Precision.HIGHEST, preferred_element_type=jnp.float32)
        nsum[d : d + 1] = line[0:1]
    core_norm = remote(nsum, n0, n0_send, n0_recv, {"core": 1 - core})
    core_norm.start()
    core_norm.wait()
    nsum[...] = nsum[...] + n0[...]
    for i, (dx, dy) in enumerate(plane):
        plane_norm(i, dx, dy).start()
    own = pl.ds((core * nx + x) * share, share)
    total = acc[own, pl.ds(pl.multiple_of(y * home, home), home)]
    for i in range(len(level)):
        level_part(i).wait_recv()
        total = total + r1[i].astype(jnp.float32)
    mags[own] = jnp.sqrt(total[:, :, :WINDOW] ** 2 + total[:, :, WINDOW:] ** 2)

    def tpl_part(i, dx, dc):
        return remote(mags.at[own], mags.at[own], r2_send.at[i], r2_recv.at[i], at_level(dx, 0, dc))

    def tpl_landed(i, dx, dc):
        spot = (lax.rem(core + dc, 2) * nx + lax.rem(x + nx - dx, nx)) * share
        ref = mags.at[pl.ds(spot, share)]
        remote(ref, ref, r2_send.at[i], r2_recv.at[i], at_level(dx, 0, dc)).wait_recv()

    for i, (dx, dc) in enumerate(tpl):
        tpl_part(i, dx, dc).start()
    table = nsum[...]
    for i, (dx, dy) in enumerate(plane):
        plane_norm(i, dx, dy).wait_recv()
        table = table + n1[i]
    info = meta[...]
    det = info[:, 0:1]
    chosen = jnp.where(det == 0, table[0:1], jnp.where(det == 1, table[1:2], table[2:3]))
    place = iota((home, names), 1)
    roots = {}
    for k in range(triggers):
        grp = info[:, 5 + k : 6 + k]
        spot = per_group * (lax.rem(grp, nz) * ny + lax.div(grp, nz))
        for m in range(per_group):
            value = jnp.sum(jnp.where(place == spot + m, chosen, 0.0), axis=1, keepdims=True)
            roots[m * triggers + k] = jnp.sqrt(value + EPSILON)
    for i, (dx, dc) in enumerate(tpl):
        tpl_landed(i, dx, dc)
    width = snr.shape[-1]
    turn = lax.rem(WINDOW - (x * 2 + core) * width, WINDOW)
    tops = jnp.zeros((home, pairs), jnp.float32)
    for k in range(triggers):
        for m in range(per_group):
            ratio = mags[m * triggers + k] / roots[m * triggers + k]
            top = jnp.max(mags[m * triggers + k], axis=1, keepdims=True) / roots[m * triggers + k]
            snr[:, k, m, :] = pltpu.roll(ratio, turn, 1)[:, :width]
            tops = jnp.where(iota((home, pairs), 1) == k * per_group + m, top, tops)
    peak[...] = tops

    for shift in range(1, ny):
        remote(stage_b.at[pl.ds(0, blocks)], stage_b.at[pl.ds(0, blocks)], yb_send.at[shift - 1],
               yb_recv.at[0, shift - 1], {"y": other_y(shift)}).wait_send()
        meta_part(shift).wait_send()
        remote(stage_s.at[shift - 1], stage_s.at[shift - 1], ys_send.at[shift - 1],
               ys_recv.at[0, shift - 1], {"y": other_y(shift)}).wait_send()
    for way in range(2):
        for h in range(1, reach + 1):
            ref = bank_buf.at[:, 0] if h < reach else bank_buf.at[pl.ds(0, blocks // 2), 0]
            remote(ref, ref, z_send.at[way, h - 1], z_recv.at[way, h - 1, 0], {"z": up}).wait_send()
    for i in range(len(level)):
        level_part(i).wait_send()
    for i, (dx, dy) in enumerate(plane):
        plane_norm(i, dx, dy).wait_send()
    for i, (dx, dc) in enumerate(tpl):
        tpl_part(i, dx, dc).wait_send()


def filter_bins(dims, strain, bank, dets, offs, names_in, wgt):
    nx, ny, nz = dims
    home, whole_blocks = strain.shape[0], strain.shape[1]
    per_group = bank.shape[0]
    blocks = whole_blocks // ny
    chunks = blocks // 2
    segs, triggers = home * ny, 4
    rows = segs * triggers
    names = nz * ny * per_group
    pairs = per_group * triggers
    share = pairs // (2 * nx)
    near = nx * ny - 1
    level = 2 * nx * ny - 1
    reach = nz // 2
    width = WINDOW // (2 * nx)
    f32, bf16 = jnp.float32, jnp.bfloat16
    dma = pltpu.SemaphoreType.DMA
    total = rows * per_group
    any_space = pl.BlockSpec(memory_space=pl.ANY)
    vmem = pl.BlockSpec(memory_space=pltpu.VMEM)
    return pl.pallas_call(
        functools.partial(filter_kernel, dims),
        in_specs=[any_space, any_space, vmem, vmem, vmem, vmem],
        out_specs=[vmem, vmem],
        out_shape=[
            jax.ShapeDtypeStruct((home, triggers, per_group, width), f32),
            jax.ShapeDtypeStruct((home, pairs), f32),
        ],
        scratch_shapes=[
            pltpu.VMEM((whole_blocks, per_group, 2, LANES), bf16),
            pltpu.VMEM((ny - 1, blocks, home, 2, LANES), bf16),
            pltpu.VMEM((blocks, nz, ny * per_group, 2, LANES), bf16),
            pltpu.VMEM((blocks, segs, 2, LANES), bf16),
            pltpu.VMEM((home, LANES), jnp.int32),
            pltpu.VMEM((ny, home, LANES), jnp.int32),
            pltpu.VMEM((2, total, 2 * names), bf16),
            pltpu.VMEM((2 * segs, 2 * segs), bf16),
            pltpu.VMEM((2, rows, CHUNK), f32),
            pltpu.VMEM((2, rows, LANES), f32),
            pltpu.VMEM((2, CHUNK, WINDOW), f32),
            pltpu.VMEM((2, chunks, WINDOW), f32),
            pltpu.VMEM((pairs, segs, 2 * WINDOW), f32),
            pltpu.VMEM((pairs, segs, 2 * WINDOW), bf16),
            pltpu.VMEM((wgt.shape[0], 2 * names, LANES), f32),
            pltpu.VMEM((8, names), f32),
            pltpu.VMEM((8, names), f32),
            pltpu.VMEM((level, share, home, 2 * WINDOW), bf16),
            pltpu.VMEM((near, 8, names), f32),
            pltpu.VMEM((pairs, home, WINDOW), f32),
            dma, dma, dma((ny,)),
            dma((ny - 1,)), dma((BANK_PARTS, ny - 1)),
            dma((ny - 1,)), dma((SEG_PARTS, ny - 1)),
            dma((ny - 1,)), dma((ny - 1,)),
            dma((2, reach)), dma((2, reach, chunks // PIECE)),
            dma, dma, dma((near,)), dma((near,)), dma((level,)), dma((level,)),
            dma((2 * nx - 1,)), dma((2 * nx - 1,)),
        ],
        compiler_params=pltpu.CompilerParams(
            collective_id=0, has_side_effects=True, vmem_limit_bytes=56 * 1024 * 1024
        ),
        cost_estimate=pl.CostEstimate(
            flops=2 * total * blocks * LANES * 1024, bytes_accessed=4 << 20, transcendentals=0
        ),
    )(strain, bank, dets, offs, names_in, wgt)


def body(dims, strain, templates, weights, detectors, offsets, routes):
    home, triggers = routes.shape

    def by_blocks(a):
        return a.reshape(a.shape[0], 2, -1, LANES).transpose(0, 2, 1, 3)

    snr, peak = filter_bins(
        dims, by_blocks(strain), by_blocks(templates), detectors[None, :], offsets.T, routes.T, weights
    )
    return snr, peak.reshape(home, triggers, -1)


def solution(mesh):
    devices = mesh.devices
    ny = 4 if devices.shape[0] % 4 == 0 and devices.shape[0] > 8 else 2
    nz = devices.shape[0] // ny
    nx = devices.shape[1] // 2
    fine = Mesh(devices.reshape(ny, nz, nx, 2), ("y", "z", "x", "core"))
    grp, tpl = ("y", "z"), ("x", "core")
    return jax.shard_map(
        functools.partial(body, (nx, ny, nz)),
        mesh=fine,
        in_specs=(
            P(grp, None, tpl),
            P(grp, None, tpl),
            P(None, tpl),
            P(grp),
            P(grp, None),
            P(grp, None),
        ),
        out_specs=(P(grp, None, None, tpl), P(grp, None, None)),
        check_vma=False,
    )
```
